128 devices in a mesh: wn: 8 (over z_hi, y), sp: 16 (over z_lo, x, core).
Axes of the slice: x: 4, y: 4, z: 4 (z_hi: 2, z_lo: 2; z = z_hi * 2 + z_lo), core: 2. Of those that a mesh axis runs over, the one named last changes fastest.
Arguments:
- adjoint: float32 [3, 16, 512, 2048], P(None, None, 'wn', 'sp'), may hold values from -6 to 6
- base_flow: float32 [3, 16, 512, 2048], P(None, None, 'wn', 'sp'), may hold values from -6 to 6
- metric: float32 [512], P('wn'), may hold values from 0.25 to 2
- propagator: float32 [512, 512], replicated
- sensor_cell: int32 [16384], P(('wn', 'sp')), may hold values from 0 to 65535
- stream_stress: float32 [16384], P(('wn', 'sp')), may hold values from -6 to 6
- span_stress: float32 [16384], P(('wn', 'sp')), may hold values from -6 to 6
- sensor_count: int32 [128], P(('wn', 'sp')), may hold values from 32 to 128, as said below
Outputs:
- updated: float32 [3, 16, 512, 2048], P(None, None, 'wn', 'sp')
The draws below stay inside these ranges and needn't reach their ends.
Inputs may be any that keep to these rules, and one draw needn't show every extreme that they name: `sensor_count`: live sensor slots of a device; the most is reached by some device.
All inputs are finite; a program needn't handle non-finite values.
Results may differ from the reference program's by a relative error of at most 0.00007.
Values sent between devices are 32-bit elements; how exact they have to be, the bound alone decides.
A program may use at most 128 MiB of HBM per device.

```python
import math
import jax
import jax.numpy as jnp
from jax import lax

NY = 512
NX = 16
SENS_DEV = 128
NZ = 2048
SENSORS = 16384


def draw_propagator(key, part):
    key = jax.random.fold_in(key, 11)
    index_y = jnp.arange(NY).astype(jnp.float32)
    spacing = jnp.abs(index_y[:, None] - index_y[None, :])
    envelope = jnp.exp(-spacing / (NY / 4.0))
    factor = jax.random.uniform(key, (NY, NY), jnp.float32, 0.5, 1.5)
    return 0.5 * jnp.eye(NY, dtype=jnp.float32) + envelope * factor / (0.4 * NY)


def draw_sensor_count(key, part):
    key = jax.random.fold_in(key, 23)
    devices_all = SENSORS // SENS_DEV
    first_key, second_key = jax.random.split(key)
    shifts = jax.random.randint(first_key, (devices_all,), 0, 3)
    counts = jnp.right_shift(jnp.full((devices_all,), SENS_DEV, jnp.int32), shifts.astype(jnp.int32))
    busiest = jax.random.randint(second_key, (), 0, devices_all)
    return counts.at[busiest].set(SENS_DEV).astype(jnp.int32)


def with_ends(entries, rng, low, top_value):
    longest = entries.shape.index(max(entries.shape))
    spots = []
    for shift in (0, 1):
        where = [jax.random.randint(jax.random.fold_in(rng, axis), (), 0, length) for axis, length in enumerate(entries.shape)]
        where[longest] = (where[longest] + shift) % entries.shape[longest]
        spots.append(tuple(where))
    return entries.at[spots[0]].set(low).at[spots[1]].set(top_value)


def steps_of(own_key, extent, shards, smallest, largest):
    def one(axis_at, shards_of):
        heights = jax.random.uniform(jax.random.fold_in(jax.random.fold_in(own_key, 6), axis_at), (shards_of,), jnp.float32, smallest / len(shards), largest / len(shards))
        return jnp.repeat(jnp.exp(heights), extent[axis_at] // shards_of).reshape((-1,) + (1,) * (len(extent) - axis_at - 1))

    level = one(*shards[0])
    for cut in shards[1:]:
        level = level * one(*cut)
    return level


def centred(key, dims, scale, reach, pieces=(), held_as=jnp.bfloat16):
    values = jax.random.normal(key, dims, jnp.float32) * scale
    if len(pieces) > 0:
        values = steps_of(key, dims, pieces, -0.22, 0.18) * values
    return jnp.clip(values, min=-reach, max=reach).astype(held_as)


def setup_inputs(seed: int = 0) -> dict:
    key_list = jax.random.split(jax.random.key(seed), 9)
    adjoint = centred(key_list[0], (3, NX, NY, NZ), 1.0, 6.0, ((2, 8), (3, 16)), jnp.float32)
    base_flow = centred(key_list[1], (3, NX, NY, NZ), 1.0, 6.0, ((2, 8), (3, 16)), jnp.float32)
    metric = jnp.clip(jnp.exp(math.log(2.0) - 2.0794415 * jax.random.uniform(key_list[2], (NY,), jnp.float32) ** steps_of(key_list[2], (NY,), ((0, 8),), -0.2, 0.2)), 0.25, 2.0)
    propagator = draw_propagator(jax.random.fold_in(key_list[8], 71), 0)
    sensor_cell = with_ends(jax.random.randint(key_list[4], (SENSORS,), 0, 2 * NX * NZ), jax.random.fold_in(key_list[4], 1), 0, (2 * NX * NZ) - 1).astype(jnp.int32)
    stream_stress = centred(key_list[5], (SENSORS,), 1.0, 6.0, ((0, 128),), jnp.float32)
    span_stress = centred(key_list[6], (SENSORS,), 1.0, 6.0, ((0, 128),), jnp.float32)
    sensor_count = draw_sensor_count(jax.random.fold_in(key_list[8], 71), 0)
    return {"adjoint": adjoint, "base_flow": base_flow, "metric": metric, "propagator": propagator, "sensor_cell": sensor_cell, "stream_stress": stream_stress, "span_stress": span_stress, "sensor_count": sensor_count}


streamwise_scale = 0.5
spanwise_scale = 0.5
time_step = 0.25


def tendency(adjoint, base_flow, gradients):
    advect = base_flow[0] * gradients[0][:3] + base_flow[1] * gradients[1][:3] + base_flow[2] * gradients[2][:3]
    stretch = jnp.stack([
        jnp.sum(adjoint * gradients[0][3:], 0),
        jnp.sum(adjoint * gradients[1][3:], 0),
        jnp.sum(adjoint * gradients[2][3:], 0)])
    return adjoint + time_step * (advect - stretch)


def reference(adjoint, base_flow, metric, propagator, sensor_cell, stream_stress, span_stress, sensor_count):
    stacked = jnp.concatenate([adjoint, base_flow], 0)
    grad_x = (jnp.roll(stacked, -1, 1) - jnp.roll(stacked, 1, 1)) * streamwise_scale
    padded = jnp.pad(stacked, ((0, 0), (0, 0), (1, 1), (0, 0)))
    grad_y = (padded[:, :, 2:, :] - padded[:, :, :-2, :]) * metric[None, None, :, None]
    grad_z = (jnp.roll(stacked, -1, 3) - jnp.roll(stacked, 1, 3)) * spanwise_scale
    forcing = tendency(adjoint, base_flow, (grad_x, grad_y, grad_z))
    slots = jnp.arange(SENSORS, dtype=jnp.int32)
    owner = slots // SENS_DEV
    alive_slot = (slots - owner * SENS_DEV) < sensor_count[owner]
    wall_side = sensor_cell // (NX * NZ)
    remainder = sensor_cell % (NX * NZ)
    plane_x = remainder // NZ
    cell_z = remainder % NZ
    row_pos = jnp.where(wall_side == 0, 1, NY - 2).astype(jnp.int32)
    forcing = forcing.at[0, plane_x, row_pos, cell_z].add(jnp.where(alive_slot, stream_stress, 0.0))
    forcing = forcing.at[2, plane_x, row_pos, cell_z].add(jnp.where(alive_slot, span_stress, 0.0))
    return jnp.einsum('yk,cxkz->cxyz', propagator, forcing, precision=lax.Precision.HIGHEST)
```

```python
import jax
import jax.numpy as jnp
from jax import lax
from jax.experimental import pallas as pl
from jax.experimental.pallas import tpu as pltpu
from jax.sharding import PartitionSpec as P

MESH = pl.DeviceIdType.MESH
BF16 = jnp.bfloat16
F32 = jnp.float32

NF = 6
PAD = 8
WN = 8
SP = 16


def kernel(
    adj_ref, base_ref, metric_ref, prop_ref, cell_ref, stream_ref, span_ref, count_ref,
    out_ref,
    fld, yh_out, yh_in, zh_out, zh_in, zh, met, send, cols, cols3, prop, prop3, rows_out,
    msg, slots, pick_rows, pick_cells, wall_part, wall_in,
    load_sem, y_send, y_recv, z_send, z_recv, f_send, f_recv, u_send, u_recv, own_sem,
    s_send, s_recv, w_send, w_recv,
):
    planes = out_ref.shape[1]
    ny = out_ref.shape[2]
    nz = out_ref.shape[3]
    tall = ny + 2 * PAD
    blocks = ny // 8
    w = lax.axis_index("wn")
    s = lax.axis_index("sp")
    lane = lax.broadcasted_iota(jnp.int32, (8, nz), 1)

    def peer(j):
        i = j // 2
        dy = (2 - i + 3 * (i // 2) - 2 * (i // 3)) % 4
        return ((w // 4 + 1 - j % 2) % 2) * 4 + (w + dy) % 4

    loads = [
        pltpu.make_async_copy(adj_ref, fld.at[pl.ds(0, 3 * planes), pl.ds(PAD, ny), :], load_sem.at[0]),
        pltpu.make_async_copy(base_ref, fld.at[pl.ds(3 * planes, 3 * planes), pl.ds(PAD, ny), :], load_sem.at[1]),
        pltpu.make_async_copy(prop_ref, prop, load_sem.at[2]),
    ]
    for load in loads:
        load.start()

    barrier = pltpu.get_barrier_semaphore()
    for j in range(WN - 1):
        pl.semaphore_signal(barrier, inc=1, device_id=(peer(j), s), device_id_type=MESH)
    for o in range(1, SP):
        pl.semaphore_signal(barrier, inc=1, device_id=(w, (s + o) % SP), device_id_type=MESH)

    alive = lax.broadcasted_iota(jnp.int32, (1, nz), 1) < count_ref[0]
    msg[...] = jnp.concatenate(
        [
            cell_ref[...].astype(F32),
            jnp.where(alive, stream_ref[...], 0.0),
            jnp.where(alive, span_ref[...], 0.0),
            jnp.zeros((5, nz), F32),
        ],
        0,
    )
    here = lax.broadcasted_iota(jnp.int32, (ny, ny), 0) == lax.broadcasted_iota(jnp.int32, (ny, ny), 1)
    column = jnp.sum(jnp.where(here, jnp.broadcast_to(metric_ref[...], (ny, ny)), 0.0), 1, keepdims=True)
    met[...] = jnp.broadcast_to(column, (ny, nz))

    loads[0].wait()
    loads[1].wait()
    flat = fld.reshape(NF * planes * tall, nz)
    yh_out[0] = flat[pl.ds(PAD + ny - 1, NF * planes, stride=tall), :]
    yh_out[1] = flat[pl.ds(PAD, NF * planes, stride=tall), :]

    def pack(r, carry):
        at = pl.multiple_of(r * 8, 8)
        for half in range(2):
            edge = jnp.zeros((8, nz), F32)
            for i in range(3 * planes):
                tile = fld[half * 3 * planes + i, pl.ds(PAD + at, 8), :]
                edge = jnp.where(lane // 2 == i, pltpu.roll(tile, 2 * i + 1, 1), edge)
            zh_out[half, pl.ds(at, 8), :] = edge
        return carry

    lax.fori_loop(0, blocks, pack, 0)

    pl.semaphore_wait(barrier, WN - 1 + SP - 1)

    halo = []
    for side in range(2):
        step = 1 - 2 * side
        halo.append(pltpu.make_async_remote_copy(
            zh_out, zh_in.at[side], z_send.at[side], z_recv.at[side],
            device_id=(w, (s + step) % SP), device_id_type=MESH))
        halo.append(pltpu.make_async_remote_copy(
            yh_out.at[side], yh_in.at[side], y_send.at[side], y_recv.at[side],
            device_id=((w + step) % WN, s), device_id_type=MESH))
    for copy in halo:
        copy.start()
    slot_copies = [
        pltpu.make_async_remote_copy(
            msg, slots.at[o], s_send.at[o], s_recv.at[o],
            device_id=(w, (s + o) % SP), device_id_type=MESH)
        for o in range(1, SP)
    ]
    for copy in slot_copies:
        copy.start()
    slots[0] = msg[...]

    depth = prop.shape[1]
    loads[2].wait()
    whole = prop[...]
    high = whole.astype(BF16)
    prop3[:, pl.ds(0, depth)] = high
    prop3[:, pl.ds(depth, depth)] = (whole - high.astype(F32)).astype(BF16)
    prop3[:, pl.ds(2 * depth, depth)] = high

    for copy in halo:
        copy.wait()
    flat[pl.ds(PAD - 1, NF * planes, stride=tall), :] = jnp.where(w == 0, 0.0, yh_in[0])
    flat[pl.ds(PAD + ny, NF * planes, stride=tall), :] = jnp.where(w == WN - 1, 0.0, yh_in[1])
    odd = lax.broadcasted_iota(jnp.int32, (ny, nz), 1) % 2 == 1
    for half in range(2):
        zh[half] = jnp.where(odd, zh_in[1, half], pltpu.roll(zh_in[0, half], 2, 1))

    def forcing(x, put):
        ahead, behind = (x + 1) % planes, (x + planes - 1) % planes

        def block(r, carry):
            at = pl.multiple_of(r * 8, 8)
            m = met[pl.ds(at, 8), :]
            mid, gx, gy, gz = [], [], [], []
            for f in range(NF):
                t = f * planes + x
                here = fld[t, pl.ds(PAD + at, 8), :]
                mid.append(here)
                gx.append((fld[f * planes + ahead, pl.ds(PAD + at, 8), :]
                           - fld[f * planes + behind, pl.ds(PAD + at, 8), :]) * 0.5)
                gy.append((fld[t, pl.ds(PAD + 1 + at, 8), :] - fld[t, pl.ds(PAD - 1 + at, 8), :]) * m)
                ends = pltpu.roll(zh[f // 3, pl.ds(at, 8), :], nz - 2 - 2 * ((f % 3) * planes + x), 1)
                gz.append((jnp.where(lane == nz - 1, ends, pltpu.roll(here, nz - 1, 1))
                           - jnp.where(lane == 0, ends, pltpu.roll(here, 1, 1))) * 0.5)
            for c in range(3):
                advect = mid[3] * gx[c] + mid[4] * gy[c] + mid[5] * gz[c]
                grad = (gx, gy, gz)[c]
                stretch = mid[0] * grad[3] + mid[1] * grad[4] + mid[2] * grad[5]
                put(at, c, mid[c] + 0.25 * (advect - stretch))
            return carry

        lax.fori_loop(0, blocks, block, 0)

    def columns_copy(k, j):
        return pltpu.make_async_remote_copy(
            send.at[k, j], cols.at[k, pl.ds(pl.multiple_of(w * ny, ny), ny), :],
            f_send.at[k, j], f_recv.at[k, j],
            device_id=(peer(j), s), device_id_type=MESH)

    def chunk(k):
        def to(j, carry):
            def put(at, c, value):
                send[k, j, pl.ds(at, 8), pl.ds(c * nz, nz)] = value

            forcing(2 * peer(j) + k, put)
            columns_copy(k, j).start()
            return carry

        lax.fori_loop(0, WN - 1, to, 0)

        def put(at, c, value):
            cols[k, pl.ds(pl.multiple_of(w * ny, ny) + at, 8), pl.ds(c * nz, nz)] = value

        forcing(2 * w + k, put)

    chunk(0)

    for copy in slot_copies:
        copy.wait()
    for i in range(SP):
        got = slots[i]
        cell = got[0:1].astype(jnp.int32)
        side = cell // (planes * nz * SP)
        left = cell % (planes * nz * SP)
        key = (left // (nz * SP)) * 2 + side
        spot = left % (nz * SP) - s * nz
        row = lax.broadcasted_iota(jnp.int32, (4 * planes, nz), 0)
        parts = [got[1:2], got[2:3]]
        for p in range(3):
            tops = [v.astype(BF16).astype(F32) for v in parts]
            parts = [v - t for v, t in zip(parts, tops)]
            pick = jnp.where(row // 2 == key, jnp.where(row % 2 == 0, tops[0], tops[1]), 0.0)
            pick_rows[pl.ds(p * 4 * planes, 4 * planes), pl.ds(i * nz, nz)] = pick.astype(BF16)
        cells = lax.broadcasted_iota(jnp.int32, (nz, nz), 0)
        pick_cells[:, pl.ds(i * nz, nz)] = jnp.where(cells == spot, 1.0, 0.0).astype(BF16)
    summed = lax.dot_general(
        pick_rows[...], pick_cells[...], (((1,), (1,)), ((), ())), preferred_element_type=F32)
    n = 4 * planes
    wall_part[...] = summed[0:n] + summed[n:2 * n] + summed[2 * n:3 * n]
    wall_copies = [
        pltpu.make_async_remote_copy(
            wall_part.at[pl.ds(pl.multiple_of(peer(j) * 8, 8), 8), :], wall_in.at[j],
            w_send.at[j], w_recv.at[j], device_id=(peer(j), s), device_id_type=MESH)
        for j in range(WN - 1)
    ]
    for copy in wall_copies:
        copy.start()
    wall_in[WN - 1] = wall_part[pl.ds(pl.multiple_of(w * 8, 8), 8), :]

    chunk(1)

    for copy in wall_copies:
        copy.wait()
    walls = wall_in[0]
    for j in range(1, WN):
        walls = walls + wall_in[j]

    def rows_copy(k, j):
        to = peer(j)
        return pltpu.make_async_remote_copy(
            rows_out.at[k, :, pl.ds(pl.multiple_of(to * ny, ny), ny), :], out_ref.at[:, 2 * w + k],
            u_send.at[k, j], u_recv.at[k, j], device_id=(to, s), device_id_type=MESH)

    own = []
    for k in range(2):
        for j in range(WN - 1):
            columns_copy(k, j).wait_recv()
        for side, y in ((0, 1), (1, depth - 2)):
            for comp, c in ((0, 0), (1, 2)):
                at = k * 4 + side * 2 + comp
                spot = (k, pl.ds(y, 1), pl.ds(c * nz, nz))
                cols[spot] = cols[spot] + walls[at:at + 1]
        whole = cols[k]
        high = whole.astype(BF16)
        cols3[pl.ds(0, depth), :] = high
        cols3[pl.ds(depth, depth), :] = high
        cols3[pl.ds(2 * depth, depth), :] = (whole - high.astype(F32)).astype(BF16)
        updated = jnp.dot(prop3[...], cols3[...], preferred_element_type=F32)
        for c in range(3):
            rows_out[k, c] = updated[:, c * nz:(c + 1) * nz]
        for j in range(WN - 1):
            rows_copy(k, j).start()
        copy = pltpu.make_async_copy(
            rows_out.at[k, :, pl.ds(pl.multiple_of(w * ny, ny), ny), :], out_ref.at[:, 2 * w + k],
            own_sem.at[k])
        copy.start()
        own.append(copy)
    for k in range(2):
        for j in range(WN - 1):
            columns_copy(k, j).wait_send()
            rows_copy(k, j).wait()
        own[k].wait()


def per_device(
    adjoint, base_flow, metric, propagator, sensor_cell, stream_stress, span_stress, sensor_count
):
    comps, planes, ny, nz = adjoint.shape
    depth = propagator.shape[0]
    vmem = pl.BlockSpec(memory_space=pltpu.VMEM)
    anywhere = pl.BlockSpec(memory_space=pl.ANY)
    dma = pltpu.SemaphoreType.DMA
    return pl.pallas_call(
        kernel,
        name="substep",
        out_shape=jax.ShapeDtypeStruct(adjoint.shape, F32),
        in_specs=[anywhere, anywhere, vmem, anywhere, vmem, vmem, vmem,
                  pl.BlockSpec(memory_space=pltpu.SMEM)],
        out_specs=anywhere,
        scratch_shapes=[
            pltpu.VMEM((NF * planes, ny + 2 * PAD, nz), F32),
            pltpu.VMEM((2, NF * planes, nz), F32),
            pltpu.VMEM((2, NF * planes, nz), F32),
            pltpu.VMEM((2, ny, nz), F32),
            pltpu.VMEM((2, 2, ny, nz), F32),
            pltpu.VMEM((2, ny, nz), F32),
            pltpu.VMEM((ny, nz), F32),
            pltpu.VMEM((2, WN - 1, ny, comps * nz), F32),
            pltpu.VMEM((2, depth, comps * nz), F32),
            pltpu.VMEM((3 * depth, comps * nz), BF16),
            pltpu.VMEM((depth, depth), F32),
            pltpu.VMEM((depth, 3 * depth), BF16),
            pltpu.VMEM((2, comps, depth, nz), F32),
            pltpu.VMEM((8, nz), F32),
            pltpu.VMEM((SP, 8, nz), F32),
            pltpu.VMEM((12 * planes, SP * nz), BF16),
            pltpu.VMEM((nz, SP * nz), BF16),
            pltpu.VMEM((4 * planes, nz), F32),
            pltpu.VMEM((WN, 8, nz), F32),
            dma((3,)),
            dma((2,)), dma((2,)), dma((2,)), dma((2,)),
            dma((2, WN - 1)), dma((2, WN - 1)), dma((2, WN - 1)), dma((2, WN - 1)),
            dma((2,)),
            dma((SP,)), dma((SP,)), dma((WN - 1,)), dma((WN - 1,)),
        ],
        compiler_params=pltpu.CompilerParams(
            collective_id=0, has_side_effects=True, vmem_limit_bytes=48 << 20),
    )(
        adjoint.reshape(comps * planes, ny, nz),
        base_flow.reshape(comps * planes, ny, nz),
        metric.reshape(1, ny),
        propagator,
        sensor_cell.reshape(1, nz),
        stream_stress.reshape(1, nz),
        span_stress.reshape(1, nz),
        sensor_count,
    )


def solution(mesh):
    placed = (
        P(None, None, "wn", "sp"),
        P(None, None, "wn", "sp"),
        P("wn"),
        P(),
        P(("wn", "sp")),
        P(("wn", "sp")),
        P(("wn", "sp")),
        P(("wn", "sp")),
    )
    return jax.shard_map(
        per_device, mesh=mesh, in_specs=placed, out_specs=P(None, None, "wn", "sp"), check_vma=False
    )
```

```python
import jax
import jax.numpy as jnp
from jax import lax
from jax.experimental import pallas as pl
from jax.experimental.pallas import tpu as pltpu
from jax.sharding import PartitionSpec as P

MESH = pl.DeviceIdType.MESH
BF16 = jnp.bfloat16
F32 = jnp.float32

NF = 6
PAD = 8
WN = 8
SP = 16


def kernel(
    adj_ref, base_ref, metric_ref, prop_ref, cell_ref, stream_ref, span_ref, count_ref,
    out_ref,
    metric_in, cell_in, stream_in, span_in,
    fld, yh_out, yh_in, zh_out, zh_in, zh, met, send, cols, cols3, prop, prop3, rows_out,
    msg, slots, pick_rows, pick_cells, wall_part, wall_in,
    load_sem, y_send, y_recv, z_send, z_recv, f_send, f_recv, u_send, u_recv, own_sem,
    s_send, s_recv, w_send, w_recv,
):
    planes = out_ref.shape[1]
    ny = out_ref.shape[2]
    nz = out_ref.shape[3]
    tall = ny + 2 * PAD
    blocks = ny // 8
    w = lax.axis_index("wn")
    s = lax.axis_index("sp")
    lane = lax.broadcasted_iota(jnp.int32, (8, nz), 1)

    def peer(j):
        i = j // 2
        dy = (2 - i + 3 * (i // 2) - 2 * (i // 3)) % 4
        return ((w // 4 + 1 - j % 2) % 2) * 4 + (w + dy) % 4

    loads = [
        pltpu.make_async_copy(adj_ref, fld.at[pl.ds(0, 3 * planes), pl.ds(PAD, ny), :], load_sem.at[0]),
        pltpu.make_async_copy(base_ref, fld.at[pl.ds(3 * planes, 3 * planes), pl.ds(PAD, ny), :], load_sem.at[1]),
        pltpu.make_async_copy(prop_ref, prop, load_sem.at[2]),
        pltpu.make_async_copy(metric_ref, metric_in, load_sem.at[3]),
        pltpu.make_async_copy(cell_ref, cell_in, load_sem.at[4]),
        pltpu.make_async_copy(stream_ref, stream_in, load_sem.at[5]),
        pltpu.make_async_copy(span_ref, span_in, load_sem.at[6]),
    ]
    for load in loads:
        load.start()

    barrier = pltpu.get_barrier_semaphore()
    for j in range(WN - 1):
        pl.semaphore_signal(barrier, inc=1, device_id=(peer(j), s), device_id_type=MESH)
    for o in range(1, SP):
        pl.semaphore_signal(barrier, inc=1, device_id=(w, (s + o) % SP), device_id_type=MESH)

    for load in loads[3:]:
        load.wait()
    alive = lax.broadcasted_iota(jnp.int32, (1, nz), 1) < count_ref[0]
    msg[...] = jnp.concatenate(
        [
            cell_in[...].astype(F32),
            jnp.where(alive, stream_in[...], 0.0),
            jnp.where(alive, span_in[...], 0.0),
            jnp.zeros((5, nz), F32),
        ],
        0,
    )
    here = lax.broadcasted_iota(jnp.int32, (ny, ny), 0) == lax.broadcasted_iota(jnp.int32, (ny, ny), 1)
    column = jnp.sum(jnp.where(here, jnp.broadcast_to(metric_in[...], (ny, ny)), 0.0), 1, keepdims=True)
    met[...] = jnp.broadcast_to(column, (ny, nz))

    loads[0].wait()
    loads[1].wait()
    flat = fld.reshape(NF * planes * tall, nz)
    yh_out[0] = flat[pl.ds(PAD + ny - 1, NF * planes, stride=tall), :]
    yh_out[1] = flat[pl.ds(PAD, NF * planes, stride=tall), :]

    def pack(r, carry):
        at = pl.multiple_of(r * 8, 8)
        for half in range(2):
            edge = jnp.zeros((8, nz), F32)
            for i in range(3 * planes):
                tile = fld[half * 3 * planes + i, pl.ds(PAD + at, 8), :]
                edge = jnp.where(lane // 2 == i, pltpu.roll(tile, 2 * i + 1, 1), edge)
            zh_out[half, pl.ds(at, 8), :] = edge
        return carry

    lax.fori_loop(0, blocks, pack, 0)

    pl.semaphore_wait(barrier, WN - 1 + SP - 1)

    halo = []
    for side in range(2):
        step = 1 - 2 * side
        halo.append(pltpu.make_async_remote_copy(
            zh_out, zh_in.at[side], z_send.at[side], z_recv.at[side],
            device_id=(w, (s + step) % SP), device_id_type=MESH))
        halo.append(pltpu.make_async_remote_copy(
            yh_out.at[side], yh_in.at[side], y_send.at[side], y_recv.at[side],
            device_id=((w + step) % WN, s), device_id_type=MESH))
    for copy in halo:
        copy.start()
    slot_copies = [
        pltpu.make_async_remote_copy(
            msg, slots.at[o], s_send.at[o], s_recv.at[o],
            device_id=(w, (s + o) % SP), device_id_type=MESH)
        for o in range(1, SP)
    ]
    for copy in slot_copies:
        copy.start()
    slots[0] = msg[...]

    depth = prop.shape[1]
    loads[2].wait()
    whole = prop[...]
    high = whole.astype(BF16)
    prop3[:, pl.ds(0, depth)] = high
    prop3[:, pl.ds(depth, depth)] = (whole - high.astype(F32)).astype(BF16)
    prop3[:, pl.ds(2 * depth, depth)] = high

    for copy in halo:
        copy.wait()
    flat[pl.ds(PAD - 1, NF * planes, stride=tall), :] = jnp.where(w == 0, 0.0, yh_in[0])
    flat[pl.ds(PAD + ny, NF * planes, stride=tall), :] = jnp.where(w == WN - 1, 0.0, yh_in[1])
    odd = lax.broadcasted_iota(jnp.int32, (ny, nz), 1) % 2 == 1
    for half in range(2):
        zh[half] = jnp.where(odd, zh_in[1, half], pltpu.roll(zh_in[0, half], 2, 1))

    def forcing(x, put):
        ahead, behind = (x + 1) % planes, (x + planes - 1) % planes

        def block(r, carry):
            at = pl.multiple_of(r * 8, 8)
            m = met[pl.ds(at, 8), :]
            mid, gx, gy, gz = [], [], [], []
            for f in range(NF):
                t = f * planes + x
                here = fld[t, pl.ds(PAD + at, 8), :]
                mid.append(here)
                gx.append((fld[f * planes + ahead, pl.ds(PAD + at, 8), :]
                           - fld[f * planes + behind, pl.ds(PAD + at, 8), :]) * 0.5)
                gy.append((fld[t, pl.ds(PAD + 1 + at, 8), :] - fld[t, pl.ds(PAD - 1 + at, 8), :]) * m)
                ends = pltpu.roll(zh[f // 3, pl.ds(at, 8), :], nz - 2 - 2 * ((f % 3) * planes + x), 1)
                gz.append((jnp.where(lane == nz - 1, ends, pltpu.roll(here, nz - 1, 1))
                           - jnp.where(lane == 0, ends, pltpu.roll(here, 1, 1))) * 0.5)
            for c in range(3):
                advect = mid[3] * gx[c] + mid[4] * gy[c] + mid[5] * gz[c]
                grad = (gx, gy, gz)[c]
                stretch = mid[0] * grad[3] + mid[1] * grad[4] + mid[2] * grad[5]
                put(at, c, mid[c] + 0.25 * (advect - stretch))
            return carry

        lax.fori_loop(0, blocks, block, 0)

    def columns_copy(k, j):
        return pltpu.make_async_remote_copy(
            send.at[k, j], cols.at[k, pl.ds(pl.multiple_of(w * ny, ny), ny), :],
            f_send.at[k, j], f_recv.at[k, j],
            device_id=(peer(j), s), device_id_type=MESH)

    def chunk(k):
        def to(j, carry):
            def put(at, c, value):
                send[k, j, pl.ds(at, 8), pl.ds(c * nz, nz)] = value

            forcing(2 * peer(j) + k, put)
            columns_copy(k, j).start()
            return carry

        lax.fori_loop(0, WN - 1, to, 0)

        def put(at, c, value):
            cols[k, pl.ds(pl.multiple_of(w * ny, ny) + at, 8), pl.ds(c * nz, nz)] = value

        forcing(2 * w + k, put)

    chunk(0)

    for copy in slot_copies:
        copy.wait()
    for i in range(SP):
        got = slots[i]
        cell = got[0:1].astype(jnp.int32)
        side = cell // (planes * nz * SP)
        left = cell % (planes * nz * SP)
        key = (left // (nz * SP)) * 2 + side
        spot = left % (nz * SP) - s * nz
        row = lax.broadcasted_iota(jnp.int32, (4 * planes, nz), 0)
        parts = [got[1:2], got[2:3]]
        for p in range(3):
            tops = [v.astype(BF16).astype(F32) for v in parts]
            parts = [v - t for v, t in zip(parts, tops)]
            pick = jnp.where(row // 2 == key, jnp.where(row % 2 == 0, tops[0], tops[1]), 0.0)
            pick_rows[pl.ds(p * 4 * planes, 4 * planes), pl.ds(i * nz, nz)] = pick.astype(BF16)
        cells = lax.broadcasted_iota(jnp.int32, (nz, nz), 0)
        pick_cells[:, pl.ds(i * nz, nz)] = jnp.where(cells == spot, 1.0, 0.0).astype(BF16)
    summed = lax.dot_general(
        pick_rows[...], pick_cells[...], (((1,), (1,)), ((), ())), preferred_element_type=F32)
    n = 4 * planes
    wall_part[...] = summed[0:n] + summed[n:2 * n] + summed[2 * n:3 * n]
    wall_copies = [
        pltpu.make_async_remote_copy(
            wall_part.at[pl.ds(pl.multiple_of(peer(j) * 8, 8), 8), :], wall_in.at[j],
            w_send.at[j], w_recv.at[j], device_id=(peer(j), s), device_id_type=MESH)
        for j in range(WN - 1)
    ]
    for copy in wall_copies:
        copy.start()
    wall_in[WN - 1] = wall_part[pl.ds(pl.multiple_of(w * 8, 8), 8), :]

    chunk(1)

    for copy in wall_copies:
        copy.wait()
    walls = wall_in[0]
    for j in range(1, WN):
        walls = walls + wall_in[j]

    def rows_copy(k, j):
        to = peer(j)
        return pltpu.make_async_remote_copy(
            rows_out.at[k, :, pl.ds(pl.multiple_of(to * ny, ny), ny), :], out_ref.at[:, 2 * w + k],
            u_send.at[k, j], u_recv.at[k, j], device_id=(to, s), device_id_type=MESH)

    own = []
    for k in range(2):
        for j in range(WN - 1):
            columns_copy(k, j).wait_recv()
        for side, y in ((0, 1), (1, depth - 2)):
            for comp, c in ((0, 0), (1, 2)):
                at = k * 4 + side * 2 + comp
                spot = (k, pl.ds(y, 1), pl.ds(c * nz, nz))
                cols[spot] = cols[spot] + walls[at:at + 1]
        whole = cols[k]
        high = whole.astype(BF16)
        cols3[pl.ds(0, depth), :] = high
        cols3[pl.ds(depth, depth), :] = high
        cols3[pl.ds(2 * depth, depth), :] = (whole - high.astype(F32)).astype(BF16)
        updated = jnp.dot(prop3[...], cols3[...], preferred_element_type=F32)
        for c in range(3):
            rows_out[k, c] = updated[:, c * nz:(c + 1) * nz]
        for j in range(WN - 1):
            rows_copy(k, j).start()
        copy = pltpu.make_async_copy(
            rows_out.at[k, :, pl.ds(pl.multiple_of(w * ny, ny), ny), :], out_ref.at[:, 2 * w + k],
            own_sem.at[k])
        copy.start()
        own.append(copy)
    for k in range(2):
        for j in range(WN - 1):
            columns_copy(k, j).wait_send()
            rows_copy(k, j).wait()
        own[k].wait()


def per_device(
    adjoint, base_flow, metric, propagator, sensor_cell, stream_stress, span_stress, sensor_count
):
    comps, planes, ny, nz = adjoint.shape
    depth = propagator.shape[0]
    hbm = pl.BlockSpec(memory_space=pltpu.HBM)
    dma = pltpu.SemaphoreType.DMA
    return pl.pallas_call(
        kernel,
        name="substep",
        out_shape=jax.ShapeDtypeStruct(adjoint.shape, F32),
        in_specs=[hbm] * 7 + [pl.BlockSpec(memory_space=pltpu.SMEM)],
        out_specs=pl.BlockSpec(memory_space=pl.ANY),
        scratch_shapes=[
            pltpu.VMEM((1, ny), F32),
            pltpu.VMEM((1, nz), jnp.int32),
            pltpu.VMEM((1, nz), F32),
            pltpu.VMEM((1, nz), F32),
            pltpu.VMEM((NF * planes, ny + 2 * PAD, nz), F32),
            pltpu.VMEM((2, NF * planes, nz), F32),
            pltpu.VMEM((2, NF * planes, nz), F32),
            pltpu.VMEM((2, ny, nz), F32),
            pltpu.VMEM((2, 2, ny, nz), F32),
            pltpu.VMEM((2, ny, nz), F32),
            pltpu.VMEM((ny, nz), F32),
            pltpu.VMEM((2, WN - 1, ny, comps * nz), F32),
            pltpu.VMEM((2, depth, comps * nz), F32),
            pltpu.VMEM((3 * depth, comps * nz), BF16),
            pltpu.VMEM((depth, depth), F32),
            pltpu.VMEM((depth, 3 * depth), BF16),
            pltpu.VMEM((2, comps, depth, nz), F32),
            pltpu.VMEM((8, nz), F32),
            pltpu.VMEM((SP, 8, nz), F32),
            pltpu.VMEM((12 * planes, SP * nz), BF16),
            pltpu.VMEM((nz, SP * nz), BF16),
            pltpu.VMEM((4 * planes, nz), F32),
            pltpu.VMEM((WN, 8, nz), F32),
            dma((7,)),
            dma((2,)), dma((2,)), dma((2,)), dma((2,)),
            dma((2, WN - 1)), dma((2, WN - 1)), dma((2, WN - 1)), dma((2, WN - 1)),
            dma((2,)),
            dma((SP,)), dma((SP,)), dma((WN - 1,)), dma((WN - 1,)),
        ],
        compiler_params=pltpu.CompilerParams(
            collective_id=0, has_side_effects=True, vmem_limit_bytes=48 << 20),
    )(
        *(pltpu.with_memory_space_constraint(a, pltpu.HBM) for a in (
            adjoint.reshape(comps * planes, ny, nz),
            base_flow.reshape(comps * planes, ny, nz),
            metric.reshape(1, ny),
            propagator,
            sensor_cell.reshape(1, nz),
            stream_stress.reshape(1, nz),
            span_stress.reshape(1, nz),
        )),
        sensor_count,
    )


def solution(mesh):
    placed = (
        P(None, None, "wn", "sp"),
        P(None, None, "wn", "sp"),
        P("wn"),
        P(),
        P(("wn", "sp")),
        P(("wn", "sp")),
        P(("wn", "sp")),
        P(("wn", "sp")),
    )
    return jax.shard_map(
        per_device, mesh=mesh, in_specs=placed, out_specs=P(None, None, "wn", "sp"), check_vma=False
    )
```

```python
import jax
import jax.numpy as jnp
from jax import lax
from jax.experimental import pallas as pl
from jax.experimental.pallas import tpu as pltpu
from jax.sharding import PartitionSpec as P

MESH = pl.DeviceIdType.MESH
BF16 = jnp.bfloat16
F32 = jnp.float32

NF = 6
PAD = 8
WN = 8
SP = 16


def kernel(
    adj_ref, base_ref, metric_ref, prop_ref, cell_ref, stream_ref, span_ref, count_ref,
    out_ref,
    metric_in, cell_in, stream_in, span_in,
    fld, yh_out, yh_in, zh_out, zh_in, fix, fix_out, fix_in, met,
    inner_out, edge_out, full_out, inner_in, edge_in, full_in, cols3, prop, prop3, rows_out,
    msg, slots, pick_rows, pick_cells, wall_part, wall_in,
    load_sem, y_send, y_recv, z_send, z_recv, x_send, x_recv, i_send, i_recv, e_send, e_recv,
    f_send, f_recv, u_send, u_recv, own_sem, s_send, s_recv, w_send, w_recv,
):
    planes = out_ref.shape[1]
    ny = out_ref.shape[2]
    nz = out_ref.shape[3]
    tall = ny + 2 * PAD
    blocks = ny // 8
    depth = prop.shape[1]
    w = lax.axis_index("wn")
    s = lax.axis_index("sp")
    lane = lax.broadcasted_iota(jnp.int32, (8, nz), 1)

    def peer(j):
        i = j // 2
        dy = (2 - i + 3 * (i // 2) - 2 * (i // 3)) % 4
        return ((w // 4 + 1 - j % 2) % 2) * 4 + (w + dy) % 4

    def to_peer(src, dst, send, recv, j):
        return pltpu.make_async_remote_copy(
            src, dst, send, recv, device_id=(peer(j), s), device_id_type=MESH)

    loads = [
        pltpu.make_async_copy(adj_ref, fld.at[pl.ds(0, 3 * planes), pl.ds(PAD, ny), :], load_sem.at[0]),
        pltpu.make_async_copy(base_ref, fld.at[pl.ds(3 * planes, 3 * planes), pl.ds(PAD, ny), :], load_sem.at[1]),
        pltpu.make_async_copy(prop_ref, prop, load_sem.at[2]),
        pltpu.make_async_copy(metric_ref, metric_in, load_sem.at[3]),
        pltpu.make_async_copy(cell_ref, cell_in, load_sem.at[4]),
        pltpu.make_async_copy(stream_ref, stream_in, load_sem.at[5]),
        pltpu.make_async_copy(span_ref, span_in, load_sem.at[6]),
    ]
    for at in (3, 4, 5, 6, 0, 1, 2):
        loads[at].start()

    barrier = pltpu.get_barrier_semaphore()
    for j in range(WN - 1):
        pl.semaphore_signal(barrier, inc=1, device_id=(peer(j), s), device_id_type=MESH)
    for o in range(1, SP):
        pl.semaphore_signal(barrier, inc=1, device_id=(w, (s + o) % SP), device_id_type=MESH)

    loads[3].wait()
    here = lax.broadcasted_iota(jnp.int32, (ny, ny), 0) == lax.broadcasted_iota(jnp.int32, (ny, ny), 1)
    column = jnp.sum(jnp.where(here, jnp.broadcast_to(metric_in[...], (ny, ny)), 0.0), 1, keepdims=True)
    met[...] = jnp.broadcast_to(2.0 * column, (ny, nz))

    for load in loads[4:]:
        load.wait()
    alive = lax.broadcasted_iota(jnp.int32, (1, nz), 1) < count_ref[0]
    msg[...] = jnp.concatenate(
        [
            cell_in[...].astype(F32),
            jnp.where(alive, stream_in[...], 0.0),
            jnp.where(alive, span_in[...], 0.0),
            jnp.zeros((5, nz), F32),
        ],
        0,
    )
    loads[0].wait()
    loads[1].wait()
    flat = fld.reshape(NF * planes * tall, nz)
    yh_out[0] = flat[pl.ds(PAD + ny - 1, NF * planes, stride=tall), :]
    yh_out[1] = flat[pl.ds(PAD, NF * planes, stride=tall), :]

    def forcing(x, at, rows, put):
        ahead, behind = (x + 1) % planes, (x + planes - 1) % planes
        m = met[pl.ds(at, rows), :]

        def read(f, plane, shift=0):
            return fld[f * planes + plane, pl.ds(PAD + shift + at, rows), :]

        mid = [read(f, x) for f in range(NF)]
        dx = [read(f, ahead) - read(f, behind) for f in range(NF)]
        dy = [read(f, x, 1) - read(f, x, -1) for f in range(NF)]
        dz = [pltpu.roll(mid[f], nz - 1, 1) - pltpu.roll(mid[f], 1, 1) for f in range(NF)]
        b1 = mid[4] * m
        for c in range(3):
            d = (dx, dy, dz)[c]
            stretch = mid[0] * d[3] + mid[1] * d[4] + mid[2] * d[5]
            if c == 1:
                stretch = stretch * m
            advect = mid[3] * dx[c] + b1 * dy[c] + mid[5] * dz[c]
            put(c, mid[c] + 0.125 * (advect - stretch))

    def fill(ref, x, first, rows):
        def put(c, value):
            ref[:, pl.ds(c * nz, nz)] = value

        forcing(x, first, rows, put)

    def fill_edges(ref, x):
        for at, to in ((0, 0), (ny - 8, 8)):
            def put(c, value, to=to):
                ref[pl.ds(to, 8), pl.ds(c * nz, nz)] = value

            forcing(x, at, 8, put)

    def inner_copy(j):
        return to_peer(inner_out.at[j], inner_in.at[w], i_send.at[j], i_recv.at[j], j)

    def edge_copy(j):
        return to_peer(edge_out.at[j], edge_in.at[w], e_send.at[j], e_recv.at[j], j)

    def full_copy(j):
        return to_peer(full_out.at[j], full_in.at[w], f_send.at[j], f_recv.at[j], j)

    def pack(r, carry):
        at = pl.multiple_of(r * 8, 8)
        for half in range(2):
            ends = jnp.zeros((8, nz), F32)
            for i in range(3 * planes):
                tile = fld[half * 3 * planes + i, pl.ds(PAD + at, 8), :]
                ends = jnp.where(lane // 2 == i, pltpu.roll(tile, 2 * i + 1, 1), ends)
            zh_out[half, pl.ds(at, 8), :] = ends
        return carry

    lax.fori_loop(0, blocks, pack, 0)
    fill(inner_out.at[0], 2 * peer(0), 8, ny - 16)
    pl.semaphore_wait(barrier, WN - 1 + SP - 1)
    y_halo, z_halo = [], []
    for side in range(2):
        step = 1 - 2 * side
        y_halo.append(pltpu.make_async_remote_copy(
            yh_out.at[side], yh_in.at[side], y_send.at[side], y_recv.at[side],
            device_id=((w + step) % WN, s), device_id_type=MESH))
        z_halo.append(pltpu.make_async_remote_copy(
            zh_out, zh_in.at[side], z_send.at[side], z_recv.at[side],
            device_id=(w, (s + step) % SP), device_id_type=MESH))
    for copy in y_halo:
        copy.start()
    for copy in z_halo:
        copy.start()
    inner_copy(0).start()

    slot_copies = [
        pltpu.make_async_remote_copy(
            msg, slots.at[o], s_send.at[o], s_recv.at[o],
            device_id=(w, (s + o) % SP), device_id_type=MESH)
        for o in range(1, SP)
    ]
    for copy in slot_copies:
        copy.start()
    slots[0] = msg[...]

    def inner(j, carry):
        fill(inner_out.at[j], 2 * peer(j), 8, ny - 16)
        inner_copy(j).start()
        return carry

    lax.fori_loop(1, WN - 1, inner, 0)
    fill(inner_in.at[w], 2 * w, 8, ny - 16)

    for copy in y_halo:
        copy.wait()
    flat[pl.ds(PAD - 1, NF * planes, stride=tall), :] = jnp.where(w == 0, 0.0, yh_in[0])
    flat[pl.ds(PAD + ny, NF * planes, stride=tall), :] = jnp.where(w == WN - 1, 0.0, yh_in[1])

    def edge(j, carry):
        fill_edges(edge_out.at[j], 2 * peer(j))
        edge_copy(j).start()
        return carry

    lax.fori_loop(0, WN - 1, edge, 0)
    fill_edges(edge_in.at[w], 2 * w)

    for copy in z_halo:
        copy.wait()
    group = lane // (2 * planes)
    packed = []
    for r in range(blocks):
        rows = pl.ds(8 * r, 8)
        own = [zh_out[half, rows, :] for half in range(2)]
        delta = [
            0.5 * jnp.where(
                lane % 2 == 0,
                pltpu.roll(zh_in[1, half, rows, :] - own[half], nz - 1, 1),
                pltpu.roll(own[half] - zh_in[0, half, rows, :], 1, 1))
            for half in range(2)
        ]
        b2 = jnp.where(
            group == 0, pltpu.roll(own[1], nz - 4 * planes, 1),
            jnp.where(group == 1, pltpu.roll(own[1], nz - 2 * planes, 1), own[1]))
        each = own[0] * delta[1]
        stretch = each + pltpu.roll(each, 2 * planes, 1) + pltpu.roll(each, 4 * planes, 1)
        packed.append(0.25 * (b2 * delta[0] - jnp.where(group == 2, stretch, 0.0)))
    for r in range(blocks):
        fix[r] = packed[r]

    def fix_of(to):
        out = jnp.zeros((8, nz), F32)
        for r in range(blocks):
            moved = pltpu.roll(fix[r], (nz + 4 * r - 4 * to) % nz, 1)
            out = jnp.where((lane % (2 * planes)) // 4 == r, moved, out)
        return out

    fix_copies = [to_peer(fix_out.at[j], fix_in.at[w], x_send.at[j], x_recv.at[j], j) for j in range(WN - 1)]
    for j in range(WN - 1):
        fix_out[j] = fix_of(peer(j))
        fix_copies[j].start()
    fix_in[w] = fix_of(w)

    for copy in slot_copies:
        copy.wait()
    n = 4 * planes
    for i in range(SP):
        got = slots[i]
        cell = got[0:1].astype(jnp.int32)
        side = cell // (planes * nz * SP)
        left = cell % (planes * nz * SP)
        key = (left // (nz * SP)) * 2 + side
        spot = left % (nz * SP) - s * nz
        row = lax.broadcasted_iota(jnp.int32, (n, nz), 0)
        parts = [got[1:2], got[2:3]]
        for p in range(3):
            tops = [v.astype(BF16).astype(F32) for v in parts]
            parts = [v - t for v, t in zip(parts, tops)]
            pick = jnp.where(row // 2 == key, jnp.where(row % 2 == 0, tops[0], tops[1]), 0.0)
            pick_rows[pl.ds(p * n, n), pl.ds(i * nz, nz)] = pick.astype(BF16)
        cells = lax.broadcasted_iota(jnp.int32, (nz, nz), 0)
        pick_cells[:, pl.ds(i * nz, nz)] = jnp.where(cells == spot, 1.0, 0.0).astype(BF16)
    summed = lax.dot_general(
        pick_rows[...], pick_cells[...], (((1,), (1,)), ((), ())), preferred_element_type=F32)
    wall_part[...] = summed[0:n] + summed[n:2 * n] + summed[2 * n:3 * n]
    wall_copies = [
        to_peer(wall_part.at[pl.ds(pl.multiple_of(peer(j) * 8, 8), 8), :], wall_in.at[j],
                w_send.at[j], w_recv.at[j], j)
        for j in range(WN - 1)
    ]
    for copy in wall_copies:
        copy.start()
    wall_in[WN - 1] = wall_part[pl.ds(pl.multiple_of(w * 8, 8), 8), :]

    def full(j, carry):
        fill(full_out.at[j], 2 * peer(j) + 1, 0, ny)
        full_copy(j).start()
        return carry

    lax.fori_loop(0, WN - 1, full, 0)
    fill(full_in.at[w], 2 * w + 1, 0, ny)

    loads[2].wait()
    whole = prop[...]
    high = whole.astype(BF16)
    prop3[:, pl.ds(0, depth)] = high
    prop3[:, pl.ds(depth, depth)] = (whole - high.astype(F32)).astype(BF16)
    prop3[:, pl.ds(2 * depth, depth)] = high

    def rows_copy(k, j):
        return to_peer(
            rows_out.at[k, :, pl.ds(pl.multiple_of(peer(j) * ny, ny), ny), :], out_ref.at[:, 2 * w + k],
            u_send.at[k, j], u_recv.at[k, j], j)

    own_copies = []
    for k in range(2):
        if k == 0:
            for j in range(WN - 1):
                inner_copy(j).wait_recv()
            for j in range(WN - 1):
                edge_copy(j).wait_recv()
            for copy in fix_copies + wall_copies:
                copy.wait()
            walls = wall_in[0]
            for j in range(1, WN):
                walls = walls + wall_in[j]
        else:
            for j in range(WN - 1):
                full_copy(j).wait_recv()
        ref, last = ((edge_in, 14), (full_in, ny - 2))[k]
        for side, (device, y) in enumerate(((0, 1), (WN - 1, last))):
            for comp, c in ((0, 0), (1, 2)):
                at = k * 4 + side * 2 + comp
                spot = (device, pl.ds(y, 1), pl.ds(c * nz, nz))
                ref[spot] = ref[spot] + walls[at:at + 1]

        def split(d, carry, k=k):
            if k == 0:
                ends = edge_in[d]
                whole = jnp.concatenate([ends[0:8], inner_in[d], ends[8:16]], 0)
            else:
                whole = full_in[d]
            change = fix_in[d]
            fixes = []
            for c in range(3):
                moved = [
                    pltpu.roll(change, (2 * nz - 1 - 2 * planes * c - 4 * r - 2 * k) % nz, 1)
                    for r in range(blocks)
                ]
                fixes.append(jnp.concatenate(
                    [jnp.where((lane == 0) | (lane == nz - 1), v, 0.0) for v in moved], 0))
            whole = whole + jnp.concatenate(fixes, 1)
            high = whole.astype(BF16)
            low = (whole - high.astype(F32)).astype(BF16)
            at = pl.multiple_of(d * ny, ny)
            cols3[pl.ds(at, ny), :] = high
            cols3[pl.ds(depth + at, ny), :] = high
            cols3[pl.ds(2 * depth + at, ny), :] = low
            return carry

        lax.fori_loop(0, WN, split, 0)
        updated = jnp.dot(prop3[...], cols3[...], preferred_element_type=F32)
        for c in range(3):
            rows_out[k, c] = updated[:, c * nz:(c + 1) * nz]
        for j in range(WN - 1):
            rows_copy(k, j).start()
        copy = pltpu.make_async_copy(
            rows_out.at[k, :, pl.ds(pl.multiple_of(w * ny, ny), ny), :], out_ref.at[:, 2 * w + k],
            own_sem.at[k])
        copy.start()
        own_copies.append(copy)
    for j in range(WN - 1):
        inner_copy(j).wait_send()
        edge_copy(j).wait_send()
        full_copy(j).wait_send()
    for k in range(2):
        for j in range(WN - 1):
            rows_copy(k, j).wait()
        own_copies[k].wait()


def per_device(
    adjoint, base_flow, metric, propagator, sensor_cell, stream_stress, span_stress, sensor_count
):
    comps, planes, ny, nz = adjoint.shape
    depth = propagator.shape[0]
    hbm = pl.BlockSpec(memory_space=pltpu.HBM)
    dma = pltpu.SemaphoreType.DMA
    return pl.pallas_call(
        kernel,
        name="substep",
        out_shape=jax.ShapeDtypeStruct(adjoint.shape, F32),
        in_specs=[hbm] * 7 + [pl.BlockSpec(memory_space=pltpu.SMEM)],
        out_specs=pl.BlockSpec(memory_space=pl.ANY),
        scratch_shapes=[
            pltpu.VMEM((1, ny), F32),
            pltpu.VMEM((1, nz), jnp.int32),
            pltpu.VMEM((1, nz), F32),
            pltpu.VMEM((1, nz), F32),
            pltpu.VMEM((NF * planes, ny + 2 * PAD, nz), F32),
            pltpu.VMEM((2, NF * planes, nz), F32),
            pltpu.VMEM((2, NF * planes, nz), F32),
            pltpu.VMEM((2, ny, nz), F32),
            pltpu.VMEM((2, 2, ny, nz), F32),
            pltpu.VMEM((ny // 8, 8, nz), F32),
            pltpu.VMEM((WN - 1, 8, nz), F32),
            pltpu.VMEM((WN, 8, nz), F32),
            pltpu.VMEM((ny, nz), F32),
            pltpu.VMEM((WN - 1, ny - 16, comps * nz), F32),
            pltpu.VMEM((WN - 1, 16, comps * nz), F32),
            pltpu.VMEM((WN - 1, ny, comps * nz), F32),
            pltpu.VMEM((WN, ny - 16, comps * nz), F32),
            pltpu.VMEM((WN, 16, comps * nz), F32),
            pltpu.VMEM((WN, ny, comps * nz), F32),
            pltpu.VMEM((3 * depth, comps * nz), BF16),
            pltpu.VMEM((depth, depth), F32),
            pltpu.VMEM((depth, 3 * depth), BF16),
            pltpu.VMEM((2, comps, depth, nz), F32),
            pltpu.VMEM((8, nz), F32),
            pltpu.VMEM((SP, 8, nz), F32),
            pltpu.VMEM((12 * planes, SP * nz), BF16),
            pltpu.VMEM((nz, SP * nz), BF16),
            pltpu.VMEM((4 * planes, nz), F32),
            pltpu.VMEM((WN, 8, nz), F32),
            dma((7,)),
            dma((2,)), dma((2,)), dma((2,)), dma((2,)),
            *([dma((WN - 1,))] * 8),
            dma((2, WN - 1)), dma((2, WN - 1)), dma((2,)),
            dma((SP,)), dma((SP,)), dma((WN - 1,)), dma((WN - 1,)),
        ],
        compiler_params=pltpu.CompilerParams(
            collective_id=0, has_side_effects=True, vmem_limit_bytes=48 << 20),
    )(
        *(pltpu.with_memory_space_constraint(a, pltpu.HBM) for a in (
            adjoint.reshape(comps * planes, ny, nz),
            base_flow.reshape(comps * planes, ny, nz),
            metric.reshape(1, ny),
            propagator,
            sensor_cell.reshape(1, nz),
            stream_stress.reshape(1, nz),
            span_stress.reshape(1, nz),
        )),
        sensor_count,
    )


def solution(mesh):
    placed = (
        P(None, None, "wn", "sp"),
        P(None, None, "wn", "sp"),
        P("wn"),
        P(),
        P(("wn", "sp")),
        P(("wn", "sp")),
        P(("wn", "sp")),
        P(("wn", "sp")),
    )
    return jax.shard_map(
        per_device, mesh=mesh, in_specs=placed, out_specs=P(None, None, "wn", "sp"), check_vma=False
    )
```

```python
import jax
import jax.numpy as jnp
from jax import lax
from jax.experimental import pallas as pl
from jax.experimental.pallas import tpu as pltpu
from jax.sharding import PartitionSpec as P

MESH = pl.DeviceIdType.MESH
BF16 = jnp.bfloat16
F32 = jnp.float32

MSG = 4
NF = 6
PAD = 8
WN = 8
SP = 16
BLOCK = 8


def kernel(
    adj_ref, base_ref, metric_ref, prop_ref, cell_ref, stream_ref, span_ref, count_ref,
    out_ref,
    metric_in, cell_in, stream_in, span_in,
    fld, yh_out, yh_in, zh_out, zh_in, fix, fix_out, fix_in, met,
    inner_out, edge_out, full_out, inner_in, edge_in, full_in, cols3, prop, prop3, rows_out,
    msg, slots, pick_rows, pick_cells, wall_part, wall_in,
    load_sem, pair_sem, y_send, y_recv, z_send, z_recv, x_send, x_recv, i_send, i_recv, e_send, e_recv,
    f_send, f_recv, u_send, u_recv, own_sem, s_send, s_recv, w_send, w_recv,
):
    planes = out_ref.shape[1]
    ny = out_ref.shape[2]
    nz = out_ref.shape[3]
    tall = ny + 2 * PAD
    blocks = ny // 8
    depth = prop.shape[1]
    w = lax.axis_index("wn")
    s = lax.axis_index("sp")
    lane = lax.broadcasted_iota(jnp.int32, (8, nz), 1)

    def peer(j):
        i = j // 2
        dy = (2 - i + 3 * (i // 2) - 2 * (i // 3)) % 4
        return ((w // 4 + 1 - j % 2) % 2) * 4 + (w + dy) % 4

    def to_peer(src, dst, send, recv, j):
        return pltpu.make_async_remote_copy(
            src, dst, send, recv, device_id=(peer(j), s), device_id_type=MESH)

    barrier = pltpu.get_barrier_semaphore()
    row_peers = [(w, (s // BLOCK) * BLOCK + (s + o) % BLOCK) for o in range(1, BLOCK)]
    slot_peers = [((w + o) % WN, (s + (o // WN) * BLOCK) % SP) for o in range(1, 2 * WN)]
    greeted = row_peers + slot_peers + [(w, (s + 1) % SP), (w, (s + SP - 1) % SP)]

    small = [
        pltpu.make_async_copy(src, dst, load_sem.at[i])
        for i, (src, dst) in enumerate((
            (metric_ref, metric_in), (cell_ref, cell_in), (stream_ref, stream_in), (span_ref, span_in)))
    ]
    load_prop = pltpu.make_async_copy(prop_ref, prop, load_sem.at[4])
    fields = fld.reshape(NF, planes, tall, nz)
    flat = fld.reshape(NF * planes * tall, nz)
    pairs = planes // 2

    def load_pair(i):
        at = pl.multiple_of(2 * ((peer(0) + (pairs - i) % pairs) % pairs), 2)
        return [
            pltpu.make_async_copy(
                ref.at[:, pl.ds(at, 2)],
                fields.at[pl.ds(3 * half, 3), pl.ds(at, 2), pl.ds(PAD, ny), :],
                pair_sem.at[i, half])
            for half, ref in enumerate((adj_ref, base_ref))
        ]

    def wait_pairs(first, last):
        for i in range(first, last):
            for copy in load_pair(i):
                copy.wait()

    def forcing(x, at, rows, put):
        ahead, behind = (x + 1) % planes, (x + planes - 1) % planes
        m = met[pl.ds(at, rows), :]

        def read(f, plane, shift=0):
            return fld[f * planes + plane, pl.ds(PAD + shift + at, rows), :]

        mid = [read(f, x) for f in range(NF)]
        dx = [read(f, ahead) - read(f, behind) for f in range(NF)]
        dy = [read(f, x, 1) - read(f, x, -1) for f in range(NF)]
        dz = [pltpu.roll(mid[f], nz - 1, 1) - pltpu.roll(mid[f], 1, 1) for f in range(NF)]
        b1 = mid[4] * m
        for c in range(3):
            d = (dx, dy, dz)[c]
            stretch = mid[0] * d[3] + mid[1] * d[4] + mid[2] * d[5]
            if c == 1:
                stretch = stretch * m
            advect = mid[3] * dx[c] + b1 * dy[c] + mid[5] * dz[c]
            put(c, mid[c] + 0.125 * (advect - stretch))

    def fill(ref, x, first, rows):
        def put(c, value):
            ref[:, pl.ds(c * nz, nz)] = value

        forcing(x, first, rows, put)

    def fill_edges(ref, x):
        for at, to in ((0, 0), (ny - 8, 8)):
            def put(c, value, to=to):
                ref[pl.ds(to, 8), pl.ds(c * nz, nz)] = value

            forcing(x, at, 8, put)

    def inner_copy(j):
        return to_peer(inner_out.at[j], inner_in.at[w], i_send.at[j], i_recv.at[j], j)

    def edge_copy(j):
        return to_peer(edge_out.at[j], edge_in.at[w], e_send.at[j], e_recv.at[j], j)

    def full_copy(j):
        return to_peer(full_out.at[j], full_in.at[w], f_send.at[j], f_recv.at[j], j)

    y_halo, z_halo = [], []
    for side in range(2):
        step = 1 - 2 * side
        y_halo.append(pltpu.make_async_remote_copy(
            yh_out.at[side], yh_in.at[side], y_send.at[side], y_recv.at[side],
            device_id=((w + step) % WN, s), device_id_type=MESH))
        z_halo.append(pltpu.make_async_remote_copy(
            zh_out, zh_in.at[side], z_send.at[side], z_recv.at[side],
            device_id=(w, (s + step) % SP), device_id_type=MESH))
    slot_copies = [
        pltpu.make_async_remote_copy(
            msg, slots.at[o + 1], s_send.at[o], s_recv.at[o], device_id=device, device_id_type=MESH)
        for o, device in enumerate(slot_peers)
    ]
    fix_copies = [to_peer(fix_out.at[j], fix_in.at[w], x_send.at[j], x_recv.at[j], j) for j in range(WN - 1)]
    wall_copies = [
        pltpu.make_async_remote_copy(
            wall_part.at[pl.ds(pl.multiple_of(((s + o + 1) % BLOCK) * 8, 8), 8), :], wall_in.at[o + 1],
            w_send.at[o], w_recv.at[o], device_id=device, device_id_type=MESH)
        for o, device in enumerate(row_peers)
    ]

    def greet():
        for device in greeted:
            pl.semaphore_signal(barrier, inc=1, device_id=device, device_id_type=MESH)

    def start_loads():
        small[0].start()
        for i in range(pairs):
            for copy in load_pair(i):
                copy.start()
        for copy in small[1:] + [load_prop]:
            copy.start()

    def spread_metric():
        small[0].wait()
        here = lax.broadcasted_iota(jnp.int32, (ny, ny), 0) == lax.broadcasted_iota(jnp.int32, (ny, ny), 1)
        column = jnp.sum(jnp.where(here, jnp.broadcast_to(metric_in[...], (ny, ny)), 0.0), 1, keepdims=True)
        met[...] = jnp.broadcast_to(2.0 * column, (ny, nz))

    def send_slots():
        for copy in small[1:]:
            copy.wait()
        alive = lax.broadcasted_iota(jnp.int32, (1, nz), 1) < count_ref[0]
        msg[...] = jnp.concatenate(
            [
                cell_in[...].astype(F32),
                jnp.where(alive, stream_in[...], 0.0),
                jnp.where(alive, span_in[...], 0.0),
                jnp.zeros((MSG - 3, nz), F32),
            ],
            0,
        )
        for copy in slot_copies:
            copy.start()
        slots[0] = msg[...]

    def pack_y():
        yh_out[0] = flat[pl.ds(PAD + ny - 1, NF * planes, stride=tall), :]
        yh_out[1] = flat[pl.ds(PAD, NF * planes, stride=tall), :]

    def send_y():
        for copy in y_halo:
            copy.start()

    def pack_z():
        def pack(r, carry):
            at = pl.multiple_of(r * 8, 8)
            for half in range(2):
                ends = jnp.zeros((8, nz), F32)
                for i in range(3 * planes):
                    tile = fld[half * 3 * planes + i, pl.ds(PAD + at, 8), :]
                    ends = jnp.where(lane // 2 == i, pltpu.roll(tile, 2 * i + 1, 1), ends)
                zh_out[half, pl.ds(at, 8), :] = ends
            return carry

        lax.fori_loop(0, blocks, pack, 0)

    def send_z():
        for copy in z_halo:
            copy.start()

    def inner(j, carry=0):
        fill(inner_out.at[j], 2 * peer(j), 8, ny - 16)
        inner_copy(j).start()
        return carry

    def inners(first, last):
        lax.fori_loop(first, last, inner, 0)

    def inner_own():
        fill(inner_in.at[w], 2 * w, 8, ny - 16)

    def wait_y():
        for copy in y_halo:
            copy.wait()
        flat[pl.ds(PAD - 1, NF * planes, stride=tall), :] = jnp.where(w == 0, 0.0, yh_in[0])
        flat[pl.ds(PAD + ny, NF * planes, stride=tall), :] = jnp.where(w == WN - 1, 0.0, yh_in[1])

    def edge(j, carry):
        fill_edges(edge_out.at[j], 2 * peer(j))
        edge_copy(j).start()
        return carry

    def edges():
        lax.fori_loop(0, WN - 1, edge, 0)
        fill_edges(edge_in.at[w], 2 * w)

    def send_fix():
        for copy in z_halo:
            copy.wait()
        group = lane // (2 * planes)
        for r in range(blocks):
            rows = pl.ds(8 * r, 8)
            own = [zh_out[half, rows, :] for half in range(2)]
            delta = [
                0.5 * jnp.where(
                    lane % 2 == 0,
                    pltpu.roll(zh_in[1, half, rows, :] - own[half], nz - 1, 1),
                    pltpu.roll(own[half] - zh_in[0, half, rows, :], 1, 1))
                for half in range(2)
            ]
            b2 = jnp.where(
                group == 0, pltpu.roll(own[1], nz - 4 * planes, 1),
                jnp.where(group == 1, pltpu.roll(own[1], nz - 2 * planes, 1), own[1]))
            each = own[0] * delta[1]
            stretch = each + pltpu.roll(each, 2 * planes, 1) + pltpu.roll(each, 4 * planes, 1)
            fix[r] = 0.25 * (b2 * delta[0] - jnp.where(group == 2, stretch, 0.0))

        def fix_of(to):
            out = jnp.zeros((8, nz), F32)
            for r in range(blocks):
                moved = pltpu.roll(fix[r], (nz + 4 * r - 4 * to) % nz, 1)
                out = jnp.where((lane % (2 * planes)) // 4 == r, moved, out)
            return out

        for j in range(WN - 1):
            fix_out[j] = fix_of(peer(j))
            fix_copies[j].start()
        fix_in[w] = fix_of(w)

    def full(j, carry):
        fill(full_out.at[j], 2 * peer(j) + 1, 0, ny)
        full_copy(j).start()
        return carry

    def fulls(first, last):
        lax.fori_loop(first, last, full, 0)

    def full_own():
        fill(full_in.at[w], 2 * w + 1, 0, ny)

    def send_walls():
        for copy in slot_copies:
            copy.wait()
        n = 8 * BLOCK
        for i in range(2 * WN):
            got = slots[i]
            cell = got[0:1].astype(jnp.int32)
            side = cell // (planes * nz * SP)
            left = cell % (planes * nz * SP)
            plane, z = left // (nz * SP), left % (nz * SP)
            tile = z // nz
            ours = (plane // 2 == w) & (tile // BLOCK == s // BLOCK)
            key = jnp.where(ours, (tile % BLOCK) * 4 + (plane % 2) * 2 + side, -1)
            row = lax.broadcasted_iota(jnp.int32, (n, nz), 0)
            parts = [got[1:2], got[2:3]]
            for p in range(3):
                tops = [v.astype(BF16).astype(F32) for v in parts]
                parts = [v - t for v, t in zip(parts, tops)]
                pick = jnp.where(row // 2 == key, jnp.where(row % 2 == 0, tops[0], tops[1]), 0.0)
                pick_rows[pl.ds(p * n, n), pl.ds(i * nz, nz)] = pick.astype(BF16)
            cells = lax.broadcasted_iota(jnp.int32, (nz, nz), 0)
            pick_cells[:, pl.ds(i * nz, nz)] = jnp.where(cells == z % nz, 1.0, 0.0).astype(BF16)
        summed = lax.dot_general(
            pick_rows[...], pick_cells[...], (((1,), (1,)), ((), ())), preferred_element_type=F32)
        wall_part[...] = summed[0:n] + summed[n:2 * n] + summed[2 * n:3 * n]
        for copy in wall_copies:
            copy.start()
        wall_in[0] = wall_part[pl.ds(pl.multiple_of((s % BLOCK) * 8, 8), 8), :]

    def split_prop():
        load_prop.wait()
        whole = prop[...]
        high = whole.astype(BF16)
        prop3[:, pl.ds(0, depth)] = high
        prop3[:, pl.ds(depth, depth)] = (whole - high.astype(F32)).astype(BF16)
        prop3[:, pl.ds(2 * depth, depth)] = high

    def rows_copy(k, j):
        return to_peer(
            rows_out.at[k, :, pl.ds(pl.multiple_of(peer(j) * ny, ny), ny), :], out_ref.at[:, 2 * w + k],
            u_send.at[k, j], u_recv.at[k, j], j)

    greet()
    start_loads()
    spread_metric()
    wait_pairs(0, 2)
    fill(inner_out.at[0], 2*peer(0), 8, ny-16)
    pl.semaphore_wait(barrier,  len(greeted))
    inner_copy(0).start()
    send_slots()
    wait_pairs(2, pairs)
    pack_y()
    send_y()
    inners(1, WN-1)
    pack_z()
    send_z()
    inner_own()
    wait_y()
    edges()
    send_fix()
    send_walls()
    fulls(0, WN-1)
    full_own()
    split_prop()

    own_copies = []
    for k in range(2):
        if k == 0:
            for j in range(WN - 1):
                inner_copy(j).wait_recv()
            for j in range(WN - 1):
                edge_copy(j).wait_recv()
            for copy in fix_copies + wall_copies:
                copy.wait()
            walls = wall_in[0]
            for o in range(1, BLOCK):
                walls = walls + wall_in[o]
        else:
            for j in range(WN - 1):
                full_copy(j).wait_recv()
        ref, last = ((edge_in, 14), (full_in, ny - 2))[k]
        for side, (device, y) in enumerate(((0, 1), (WN - 1, last))):
            for comp, c in ((0, 0), (1, 2)):
                at = k * 4 + side * 2 + comp
                spot = (device, pl.ds(y, 1), pl.ds(c * nz, nz))
                ref[spot] = ref[spot] + walls[at:at + 1]

        def split(d, carry, k=k):
            if k == 0:
                ends = edge_in[d]
                whole = jnp.concatenate([ends[0:8], inner_in[d], ends[8:16]], 0)
            else:
                whole = full_in[d]
            change = fix_in[d]
            fixes = []
            for c in range(3):
                moved = [
                    pltpu.roll(change, (2 * nz - 1 - 2 * planes * c - 4 * r - 2 * k) % nz, 1)
                    for r in range(blocks)
                ]
                fixes.append(jnp.concatenate(
                    [jnp.where((lane == 0) | (lane == nz - 1), v, 0.0) for v in moved], 0))
            whole = whole + jnp.concatenate(fixes, 1)
            high = whole.astype(BF16)
            low = (whole - high.astype(F32)).astype(BF16)
            at = pl.multiple_of(d * ny, ny)
            cols3[pl.ds(at, ny), :] = high
            cols3[pl.ds(depth + at, ny), :] = high
            cols3[pl.ds(2 * depth + at, ny), :] = low
            return carry

        lax.fori_loop(0, WN, split, 0)
        updated = jnp.dot(prop3[...], cols3[...], preferred_element_type=F32)
        for c in range(3):
            rows_out[k, c] = updated[:, c * nz:(c + 1) * nz]
        for j in range(WN - 1):
            rows_copy(k, j).start()
        copy = pltpu.make_async_copy(
            rows_out.at[k, :, pl.ds(pl.multiple_of(w * ny, ny), ny), :], out_ref.at[:, 2 * w + k],
            own_sem.at[k])
        copy.start()
        own_copies.append(copy)
    for j in range(WN - 1):
        inner_copy(j).wait_send()
        edge_copy(j).wait_send()
        full_copy(j).wait_send()
    for k in range(2):
        for j in range(WN - 1):
            rows_copy(k, j).wait()
        own_copies[k].wait()


def per_device(
    adjoint, base_flow, metric, propagator, sensor_cell, stream_stress, span_stress, sensor_count
):
    comps, planes, ny, nz = adjoint.shape
    depth = propagator.shape[0]
    hbm = pl.BlockSpec(memory_space=pltpu.HBM)
    dma = pltpu.SemaphoreType.DMA
    return pl.pallas_call(
        kernel,
        name="substep",
        out_shape=jax.ShapeDtypeStruct(adjoint.shape, F32),
        in_specs=[hbm] * 7 + [pl.BlockSpec(memory_space=pltpu.SMEM)],
        out_specs=pl.BlockSpec(memory_space=pl.ANY),
        scratch_shapes=[
            pltpu.VMEM((1, ny), F32),
            pltpu.VMEM((1, nz), jnp.int32),
            pltpu.VMEM((1, nz), F32),
            pltpu.VMEM((1, nz), F32),
            pltpu.VMEM((NF * planes, ny + 2 * PAD, nz), F32),
            pltpu.VMEM((2, NF * planes, nz), F32),
            pltpu.VMEM((2, NF * planes, nz), F32),
            pltpu.VMEM((2, ny, nz), F32),
            pltpu.VMEM((2, 2, ny, nz), F32),
            pltpu.VMEM((ny // 8, 8, nz), F32),
            pltpu.VMEM((WN - 1, 8, nz), F32),
            pltpu.VMEM((WN, 8, nz), F32),
            pltpu.VMEM((ny, nz), F32),
            pltpu.VMEM((WN - 1, ny - 16, comps * nz), F32),
            pltpu.VMEM((WN - 1, 16, comps * nz), F32),
            pltpu.VMEM((WN - 1, ny, comps * nz), F32),
            pltpu.VMEM((WN, ny - 16, comps * nz), F32),
            pltpu.VMEM((WN, 16, comps * nz), F32),
            pltpu.VMEM((WN, ny, comps * nz), F32),
            pltpu.VMEM((3 * depth, comps * nz), BF16),
            pltpu.VMEM((depth, depth), F32),
            pltpu.VMEM((depth, 3 * depth), BF16),
            pltpu.VMEM((2, comps, depth, nz), F32),
            pltpu.VMEM((MSG, nz), F32),
            pltpu.VMEM((2 * WN, MSG, nz), F32),
            pltpu.VMEM((24 * BLOCK, 2 * WN * nz), BF16),
            pltpu.VMEM((nz, 2 * WN * nz), BF16),
            pltpu.VMEM((8 * BLOCK, nz), F32),
            pltpu.VMEM((BLOCK, 8, nz), F32),
            dma((5,)), dma((planes // 2, 2)),
            dma((2,)), dma((2,)), dma((2,)), dma((2,)),
            *([dma((WN - 1,))] * 8),
            dma((2, WN - 1)), dma((2, WN - 1)), dma((2,)),
            dma((2 * WN - 1,)), dma((2 * WN - 1,)), dma((BLOCK - 1,)), dma((BLOCK - 1,)),
        ],
        compiler_params=pltpu.CompilerParams(
            collective_id=0, has_side_effects=True, vmem_limit_bytes=48 << 20),
    )(
        *(pltpu.with_memory_space_constraint(a, pltpu.HBM) for a in (
            adjoint,
            base_flow,
            metric.reshape(1, ny),
            propagator,
            sensor_cell.reshape(1, nz),
            stream_stress.reshape(1, nz),
            span_stress.reshape(1, nz),
        )),
        sensor_count,
    )


def solution(mesh):
    placed = (
        P(None, None, "wn", "sp"),
        P(None, None, "wn", "sp"),
        P("wn"),
        P(),
        P(("wn", "sp")),
        P(("wn", "sp")),
        P(("wn", "sp")),
        P(("wn", "sp")),
    )
    return jax.shard_map(
        per_device, mesh=mesh, in_specs=placed, out_specs=P(None, None, "wn", "sp"), check_vma=False
    )
```

```python
import jax
import jax.numpy as jnp
from jax import lax
from jax.experimental import pallas as pl
from jax.experimental.pallas import tpu as pltpu
from jax.sharding import PartitionSpec as P

MESH = pl.DeviceIdType.MESH
BF16 = jnp.bfloat16
F32 = jnp.float32

MSG = 3
NF = 6
PAD = 8
WN = 8
SP = 16
BLOCK = 8


def kernel(
    adj_ref, base_ref, metric_ref, prop_ref, cell_ref, stream_ref, span_ref, count_ref,
    out_ref,
    metric_in, cell_in, stream_in, span_in,
    fld, yh_out, yh_in, ends_own, zh_out, zh_in, fix, fix_out, fix_in, met,
    inner_out, edge_out, inner_in, edge_in, cols3, prop, prop3, rows_out,
    msg, slots, pick_rows, pick_cells, wall_part, wall_in,
    load_sem, pair_sem, y_send, y_recv, z_send, z_recv, x_send, x_recv, i_send, i_recv, e_send, e_recv,
    u_send, u_recv, own_sem, s_send, s_recv, w_send, w_recv,
):
    planes = out_ref.shape[1]
    ny = out_ref.shape[2]
    nz = out_ref.shape[3]
    tall = ny + 2 * PAD
    blocks = ny // 8
    depth = prop.shape[1]
    w = lax.axis_index("wn")
    s = lax.axis_index("sp")
    lane = lax.broadcasted_iota(jnp.int32, (8, nz), 1)

    def peer(j):
        i = j // 2
        dy = (2 - i + 3 * (i // 2) - 2 * (i // 3)) % 4
        return ((w // 4 + 1 - j % 2) % 2) * 4 + (w + dy) % 4

    def to_peer(src, dst, send, recv, j):
        return pltpu.make_async_remote_copy(
            src, dst, send, recv, device_id=(peer(j), s), device_id_type=MESH)

    barrier = pltpu.get_barrier_semaphore()
    row_peers = [(w, (s // BLOCK) * BLOCK + (s + o) % BLOCK) for o in range(1, BLOCK)]
    slot_peers = [((w + o) % WN, (s + (o // WN) * BLOCK) % SP) for o in range(1, 2 * WN)]
    greeted = row_peers + slot_peers + [(w, (s + 1) % SP), (w, (s + SP - 1) % SP)]

    small = [
        pltpu.make_async_copy(src, dst, load_sem.at[i])
        for i, (src, dst) in enumerate((
            (metric_ref, metric_in), (cell_ref, cell_in), (stream_ref, stream_in), (span_ref, span_in)))
    ]
    load_prop = pltpu.make_async_copy(prop_ref, prop, load_sem.at[4])
    fields = fld.reshape(NF, planes, tall, nz)
    flat = fld.reshape(NF * planes * tall, nz)
    pairs = planes // 2

    def load_pair(i):
        at = pl.multiple_of(2 * ((peer(0) + (pairs - i) % pairs) % pairs), 2)
        return [
            pltpu.make_async_copy(
                ref.at[:, pl.ds(at, 2)],
                fields.at[pl.ds(3 * half, 3), pl.ds(at, 2), pl.ds(PAD, ny), :],
                pair_sem.at[i, half])
            for half, ref in enumerate((adj_ref, base_ref))
        ]

    def wait_pairs(first, last):
        for i in range(first, last):
            for copy in load_pair(i):
                copy.wait()

    def forcing(x, at, rows, put):
        ahead, behind = (x + 1) % planes, (x + planes - 1) % planes
        m = met[pl.ds(at, rows), :]

        def read(f, plane, shift=0):
            return fld[f * planes + plane, pl.ds(PAD + shift + at, rows), :]

        mid = [read(f, x) for f in range(NF)]
        dx = [read(f, ahead) - read(f, behind) for f in range(NF)]
        dy = [read(f, x, 1) - read(f, x, -1) for f in range(NF)]
        dz = [pltpu.roll(mid[f], nz - 1, 1) - pltpu.roll(mid[f], 1, 1) for f in range(NF)]
        b1 = mid[4] * m
        for c in range(3):
            d = (dx, dy, dz)[c]
            stretch = mid[0] * d[3] + mid[1] * d[4] + mid[2] * d[5]
            if c == 1:
                stretch = stretch * m
            advect = mid[3] * dx[c] + b1 * dy[c] + mid[5] * dz[c]
            put(c, mid[c] + 0.125 * (advect - stretch))

    def fill(ref, x, first, rows):
        def put(c, value):
            ref[:, pl.ds(c * nz, nz)] = value

        forcing(x, first, rows, put)

    def fill_edges(ref, x):
        for at, to in ((0, 0), (ny - 8, 8)):
            def put(c, value, to=to):
                ref[pl.ds(to, 8), pl.ds(c * nz, nz)] = value

            forcing(x, at, 8, put)

    def inner_copy(k, j):
        return to_peer(inner_out.at[k, j], inner_in.at[k, w], i_send.at[k, j], i_recv.at[k, j], j)

    def edge_copy(k, j):
        return to_peer(edge_out.at[k, j], edge_in.at[k, w], e_send.at[k, j], e_recv.at[k, j], j)

    y_halo, z_halo = [], []
    for side in range(2):
        step = 1 - 2 * side
        y_halo.append(pltpu.make_async_remote_copy(
            yh_out.at[side], yh_in.at[side], y_send.at[side], y_recv.at[side],
            device_id=((w + step) % WN, s), device_id_type=MESH))
        z_halo.append(pltpu.make_async_remote_copy(
            zh_out.at[side], zh_in.at[side], z_send.at[side], z_recv.at[side],
            device_id=(w, (s + step) % SP), device_id_type=MESH))
    slot_copies = [
        pltpu.make_async_remote_copy(
            msg, slots.at[o + 1], s_send.at[o], s_recv.at[o], device_id=device, device_id_type=MESH)
        for o, device in enumerate(slot_peers)
    ]
    fix_copies = [to_peer(fix_out.at[j], fix_in.at[w], x_send.at[j], x_recv.at[j], j) for j in range(WN - 1)]
    wall_copies = [
        pltpu.make_async_remote_copy(
            wall_part.at[pl.ds(pl.multiple_of(((s + o + 1) % BLOCK) * 8, 8), 8), :], wall_in.at[o + 1],
            w_send.at[o], w_recv.at[o], device_id=device, device_id_type=MESH)
        for o, device in enumerate(row_peers)
    ]

    def greet():
        for device in greeted:
            pl.semaphore_signal(barrier, inc=1, device_id=device, device_id_type=MESH)

    def start_loads():
        small[0].start()
        for i in range(pairs):
            for copy in load_pair(i):
                copy.start()
        for copy in small[1:] + [load_prop]:
            copy.start()

    def spread_metric():
        small[0].wait()
        here = lax.broadcasted_iota(jnp.int32, (ny, ny), 0) == lax.broadcasted_iota(jnp.int32, (ny, ny), 1)
        column = jnp.sum(jnp.where(here, jnp.broadcast_to(metric_in[...], (ny, ny)), 0.0), 1, keepdims=True)
        met[...] = jnp.broadcast_to(2.0 * column, (ny, nz))

    def build_slots():
        for copy in small[1:]:
            copy.wait()
        alive = lax.broadcasted_iota(jnp.int32, (1, nz), 1) < count_ref[0]
        msg[...] = jnp.concatenate(
            [
                cell_in[...].astype(F32),
                jnp.where(alive, stream_in[...], 0.0),
                jnp.where(alive, span_in[...], 0.0),
            ],
            0,
        )
        slots[0] = msg[...]

    def start_slots():
        for copy in slot_copies:
            copy.start()

    def pack_y():
        yh_out[0] = flat[pl.ds(PAD + ny - 1, NF * planes, stride=tall), :]
        yh_out[1] = flat[pl.ds(PAD, NF * planes, stride=tall), :]

    def send_y():
        pl.when(w != WN - 1)(y_halo[0].start)
        pl.when(w != 0)(y_halo[1].start)

    def pack_z():
        def pack(r, carry):
            at = pl.multiple_of(r * 8, 8)
            halves = []
            for half in range(2):
                ends = jnp.zeros((8, nz), F32)
                for i in range(3 * planes):
                    tile = fld[half * 3 * planes + i, pl.ds(PAD + at, 8), :]
                    ends = jnp.where(lane // 2 == i, pltpu.roll(tile, 2 * i + 1, 1), ends)
                ends_own[half, pl.ds(at, 8), :] = ends
                halves.append(ends)
            even = lane % 2 == 0
            zh_out[0, pl.ds(at, 8), :] = jnp.where(even, halves[0], pltpu.roll(halves[1], 1, 1))
            zh_out[1, pl.ds(at, 8), :] = jnp.where(even, pltpu.roll(halves[1], nz - 1, 1), halves[0])
            return carry

        lax.fori_loop(0, blocks, pack, 0)

    def send_z():
        for copy in z_halo:
            copy.start()

    def fill_inner(k, j):
        fill(inner_out.at[k, j], 2 * peer(j) + k, 8, ny - 16)

    def inners(k, first, last):
        def inner(j, carry):
            fill_inner(k, j)
            inner_copy(k, j).start()
            return carry

        lax.fori_loop(first, last, inner, 0)

    def inner_own(k):
        fill(inner_in.at[k, w], 2 * w + k, 8, ny - 16)

    def wait_y():
        for side, (edge_of_wall, row) in enumerate(((0, PAD - 1), (WN - 1, PAD + ny))):
            spot = (pl.ds(row, NF * planes, stride=tall), slice(None))

            @pl.when(w != edge_of_wall)
            def _(side=side, spot=spot):
                y_halo[side].wait_recv()
                flat[spot] = yh_in[side]

            @pl.when(w == edge_of_wall)
            def _(spot=spot):
                flat[spot] = jnp.zeros((NF * planes, nz), F32)

        pl.when(w != WN - 1)(y_halo[0].wait_send)
        pl.when(w != 0)(y_halo[1].wait_send)

    def edges(k):
        def edge(j, carry):
            fill_edges(edge_out.at[k, j], 2 * peer(j) + k)
            edge_copy(k, j).start()
            return carry

        lax.fori_loop(0, WN - 1, edge, 0)
        fill_edges(edge_in.at[k, w], 2 * w + k)

    def send_fix():
        for copy in z_halo:
            copy.wait()
        group = lane // (2 * planes)
        for r in range(blocks):
            rows = pl.ds(8 * r, 8)
            own = [ends_own[half, rows, :] for half in range(2)]
            before, after = zh_in[0, rows, :], zh_in[1, rows, :]
            before = [before, pltpu.roll(before, nz - 1, 1)]
            after = [after, pltpu.roll(after, 1, 1)]
            delta = [
                0.5 * jnp.where(
                    lane % 2 == 0,
                    pltpu.roll(after[half] - own[half], nz - 1, 1),
                    pltpu.roll(own[half] - before[half], 1, 1))
                for half in range(2)
            ]
            b2 = jnp.where(
                group == 0, pltpu.roll(own[1], nz - 4 * planes, 1),
                jnp.where(group == 1, pltpu.roll(own[1], nz - 2 * planes, 1), own[1]))
            each = own[0] * delta[1]
            stretch = each + pltpu.roll(each, 2 * planes, 1) + pltpu.roll(each, 4 * planes, 1)
            fix[r] = 0.25 * (b2 * delta[0] - jnp.where(group == 2, stretch, 0.0))

        def fix_of(to):
            out = jnp.zeros((8, nz), F32)
            for r in range(blocks):
                moved = pltpu.roll(fix[r], (nz + 4 * r - 4 * to) % nz, 1)
                out = jnp.where((lane % (2 * planes)) // 4 == r, moved, out)
            return out

        for j in range(WN - 1):
            fix_out[j] = fix_of(peer(j))
            fix_copies[j].start()
        fix_in[w] = fix_of(w)

    def send_walls():
        for copy in slot_copies:
            copy.wait()
        n = 8 * BLOCK
        for i in range(2 * WN):
            got = slots[i]
            cell = got[0:1].astype(jnp.int32)
            side = cell // (planes * nz * SP)
            left = cell % (planes * nz * SP)
            plane, z = left // (nz * SP), left % (nz * SP)
            tile = z // nz
            ours = (plane // 2 == w) & (tile // BLOCK == s // BLOCK)
            key = jnp.where(ours, (tile % BLOCK) * 4 + (plane % 2) * 2 + side, -1)
            row = lax.broadcasted_iota(jnp.int32, (n, nz), 0)
            parts = [got[1:2], got[2:3]]
            for p in range(3):
                tops = [v.astype(BF16).astype(F32) for v in parts]
                parts = [v - t for v, t in zip(parts, tops)]
                pick = jnp.where(row // 2 == key, jnp.where(row % 2 == 0, tops[0], tops[1]), 0.0)
                pick_rows[pl.ds(p * n, n), pl.ds(i * nz, nz)] = pick.astype(BF16)
            cells = lax.broadcasted_iota(jnp.int32, (nz, nz), 0)
            pick_cells[:, pl.ds(i * nz, nz)] = jnp.where(cells == z % nz, 1.0, 0.0).astype(BF16)
        summed = lax.dot_general(
            pick_rows[...], pick_cells[...], (((1,), (1,)), ((), ())), preferred_element_type=F32)
        wall_part[...] = summed[0:n] + summed[n:2 * n] + summed[2 * n:3 * n]
        for copy in wall_copies:
            copy.start()
        wall_in[0] = wall_part[pl.ds(pl.multiple_of((s % BLOCK) * 8, 8), 8), :]

    def split_prop():
        load_prop.wait()
        whole = prop[...]
        high = whole.astype(BF16)
        prop3[:, pl.ds(0, depth)] = high
        prop3[:, pl.ds(depth, depth)] = (whole - high.astype(F32)).astype(BF16)
        prop3[:, pl.ds(2 * depth, depth)] = high

    def rows_copy(k, j):
        return to_peer(
            rows_out.at[k, :, pl.ds(pl.multiple_of(peer(j) * ny, ny), ny), :], out_ref.at[:, 2 * w + k],
            u_send.at[k, j], u_recv.at[k, j], j)

    greet()
    start_loads()
    spread_metric()
    wait_pairs(0, pairs)
    pack_y()
    fill_inner(0, 0)
    fill_inner(0, 1)
    build_slots()
    pl.semaphore_wait(barrier, len(greeted))
    inner_copy(0, 0).start()
    inner_copy(0, 1).start()
    send_y()
    start_slots()
    inners(0, 2, WN - 1)
    pack_z()
    send_z()
    inner_own(0)
    inners(1, 0, 2)
    wait_y()
    edges(0)
    send_fix()
    send_walls()
    inners(1, 2, WN - 1)
    edges(1)
    inner_own(1)
    split_prop()

    own_copies = []
    for k in range(2):
        for j in range(WN - 1):
            inner_copy(k, j).wait_recv()
            edge_copy(k, j).wait_recv()
        if k == 0:
            for copy in fix_copies + wall_copies:
                copy.wait()
            walls = wall_in[0]
            for o in range(1, BLOCK):
                walls = walls + wall_in[o]
        for side, (device, y) in enumerate(((0, 1), (WN - 1, 14))):
            for comp, c in ((0, 0), (1, 2)):
                at = k * 4 + side * 2 + comp
                spot = (k, device, pl.ds(y, 1), pl.ds(c * nz, nz))
                edge_in[spot] = edge_in[spot] + walls[at:at + 1]

        def split(d, carry, k=k):
            ends = edge_in[k, d]
            whole = jnp.concatenate([ends[0:8], inner_in[k, d], ends[8:16]], 0)
            change = fix_in[d]
            fixes = []
            for c in range(3):
                moved = [
                    pltpu.roll(change, (2 * nz - 1 - 2 * planes * c - 4 * r - 2 * k) % nz, 1)
                    for r in range(blocks)
                ]
                fixes.append(jnp.concatenate(
                    [jnp.where((lane == 0) | (lane == nz - 1), v, 0.0) for v in moved], 0))
            whole = whole + jnp.concatenate(fixes, 1)
            high = whole.astype(BF16)
            low = (whole - high.astype(F32)).astype(BF16)
            at = pl.multiple_of(d * ny, ny)
            cols3[pl.ds(at, ny), :] = high
            cols3[pl.ds(depth + at, ny), :] = high
            cols3[pl.ds(2 * depth + at, ny), :] = low
            return carry

        lax.fori_loop(0, WN, split, 0)
        updated = jnp.dot(prop3[...], cols3[...], preferred_element_type=F32)
        for c in range(3):
            rows_out[k, c] = updated[:, c * nz:(c + 1) * nz]
        for j in range(WN - 1):
            rows_copy(k, j).start()
        copy = pltpu.make_async_copy(
            rows_out.at[k, :, pl.ds(pl.multiple_of(w * ny, ny), ny), :], out_ref.at[:, 2 * w + k],
            own_sem.at[k])
        copy.start()
        own_copies.append(copy)
    for k in range(2):
        for j in range(WN - 1):
            inner_copy(k, j).wait_send()
            edge_copy(k, j).wait_send()
    for k in range(2):
        for j in range(WN - 1):
            rows_copy(k, j).wait()
        own_copies[k].wait()


def per_device(
    adjoint, base_flow, metric, propagator, sensor_cell, stream_stress, span_stress, sensor_count
):
    comps, planes, ny, nz = adjoint.shape
    depth = propagator.shape[0]
    hbm = pl.BlockSpec(memory_space=pltpu.HBM)
    dma = pltpu.SemaphoreType.DMA
    return pl.pallas_call(
        kernel,
        name="substep",
        out_shape=jax.ShapeDtypeStruct(adjoint.shape, F32),
        in_specs=[hbm] * 7 + [pl.BlockSpec(memory_space=pltpu.SMEM)],
        out_specs=pl.BlockSpec(memory_space=pl.ANY),
        scratch_shapes=[
            pltpu.VMEM((1, ny), F32),
            pltpu.VMEM((1, nz), jnp.int32),
            pltpu.VMEM((1, nz), F32),
            pltpu.VMEM((1, nz), F32),
            pltpu.VMEM((NF * planes, ny + 2 * PAD, nz), F32),
            pltpu.VMEM((2, NF * planes, nz), F32),
            pltpu.VMEM((2, NF * planes, nz), F32),
            pltpu.VMEM((2, ny, nz), F32),
            pltpu.VMEM((2, ny, nz), F32),
            pltpu.VMEM((2, ny, nz), F32),
            pltpu.VMEM((ny // 8, 8, nz), F32),
            pltpu.VMEM((WN - 1, 8, nz), F32),
            pltpu.VMEM((WN, 8, nz), F32),
            pltpu.VMEM((ny, nz), F32),
            pltpu.VMEM((2, WN - 1, ny - 16, comps * nz), F32),
            pltpu.VMEM((2, WN - 1, 16, comps * nz), F32),
            pltpu.VMEM((2, WN, ny - 16, comps * nz), F32),
            pltpu.VMEM((2, WN, 16, comps * nz), F32),
            pltpu.VMEM((3 * depth, comps * nz), BF16),
            pltpu.VMEM((depth, depth), F32),
            pltpu.VMEM((depth, 3 * depth), BF16),
            pltpu.VMEM((2, comps, depth, nz), F32),
            pltpu.VMEM((MSG, nz), F32),
            pltpu.VMEM((2 * WN, MSG, nz), F32),
            pltpu.VMEM((24 * BLOCK, 2 * WN * nz), BF16),
            pltpu.VMEM((nz, 2 * WN * nz), BF16),
            pltpu.VMEM((8 * BLOCK, nz), F32),
            pltpu.VMEM((BLOCK, 8, nz), F32),
            dma((5,)), dma((planes // 2, 2)),
            dma((2,)), dma((2,)), dma((2,)), dma((2,)),
            dma((WN - 1,)), dma((WN - 1,)),
            *([dma((2, WN - 1))] * 6), dma((2,)),
            dma((2 * WN - 1,)), dma((2 * WN - 1,)), dma((BLOCK - 1,)), dma((BLOCK - 1,)),
        ],
        compiler_params=pltpu.CompilerParams(
            collective_id=0, has_side_effects=True, vmem_limit_bytes=48 << 20),
    )(
        *(pltpu.with_memory_space_constraint(a, pltpu.HBM) for a in (
            adjoint,
            base_flow,
            metric.reshape(1, ny),
            propagator,
            sensor_cell.reshape(1, nz),
            stream_stress.reshape(1, nz),
            span_stress.reshape(1, nz),
        )),
        sensor_count,
    )


def solution(mesh):
    placed = (
        P(None, None, "wn", "sp"),
        P(None, None, "wn", "sp"),
        P("wn"),
        P(),
        P(("wn", "sp")),
        P(("wn", "sp")),
        P(("wn", "sp")),
        P(("wn", "sp")),
    )
    return jax.shard_map(
        per_device, mesh=mesh, in_specs=placed, out_specs=P(None, None, "wn", "sp"), check_vma=False
    )
```

```python
import jax
import jax.numpy as jnp
from jax import lax
from jax.experimental import pallas as pl
from jax.experimental.pallas import tpu as pltpu
from jax.sharding import PartitionSpec as P

MESH = pl.DeviceIdType.MESH
BF16 = jnp.bfloat16
F32 = jnp.float32

MSG = 8
NF = 6
PAD = 8
WN = 8
SP = 16
BLOCK = 8


def kernel(
    adj_ref, base_ref, metric_ref, prop_ref, cell_ref, stream_ref, span_ref, count_ref,
    out_ref,
    metric_in, cell_in, stream_in, span_in,
    fld, yh_out, yh_in, ends_own, zh_out, zh_in, fix, fix_out, fix_in, met,
    inner_out, edge_out, inner_in, edge_in, cols3, prop, prop3, rows_out,
    msg, slots, pick_rows, pick_cells, wall_part, wall_in,
    load_sem, pair_sem, y_send, y_recv, z_send, z_recv, x_send, x_recv, i_send, i_recv, e_send, e_recv,
    u_send, u_recv, own_sem, s_send, s_recv, w_send, w_recv,
):
    planes = out_ref.shape[1]
    ny = out_ref.shape[2]
    nz = out_ref.shape[3]
    tall = ny + 2 * PAD
    blocks = ny // 8
    depth = prop.shape[1]
    w = lax.axis_index("wn")
    s = lax.axis_index("sp")
    lane = lax.broadcasted_iota(jnp.int32, (8, nz), 1)
    row8 = lax.broadcasted_iota(jnp.int32, (8, nz), 0)

    mirror = 1 - 2 * lax.rem(s, 2)
    half, along = lax.div(w, 4), lax.rem(w, 4) + 4
    steps = ((2, 1), (1, 1), (-1, 0), (0, 1), (-1, 1), (1, 0), (2, 0), (0, 0))

    def peer(j):
        if isinstance(j, int):
            dy, dz = steps[j]
        else:
            dy, dz = 0, 0
            for i, (y, z) in enumerate(steps):
                dy, dz = jnp.where(j == i, y, dy), jnp.where(j == i, z, dz)
        return lax.rem(half + dz, 2) * 4 + lax.rem(along + dy * mirror, 4)

    def to_peer(src, dst, send, recv, j):
        return pltpu.make_async_remote_copy(
            src, dst, send, recv, device_id=(peer(j), s), device_id_type=MESH)

    barrier = pltpu.get_barrier_semaphore()
    base = s - lax.rem(s, BLOCK)
    row_peers = [(w, base + lax.rem(s + o, BLOCK)) for o in range(1, BLOCK)]
    across = lax.rem(s + BLOCK, SP)
    slot_peers = [(lax.rem(w + o, WN), across if o >= WN else s) for o in range(1, 2 * WN)]
    greeted = row_peers + slot_peers + [(w, lax.rem(s + 1, SP)), (w, lax.rem(s + SP - 1, SP))]

    small = [
        pltpu.make_async_copy(src, dst, load_sem.at[i])
        for i, (src, dst) in enumerate((
            (metric_ref, metric_in), (cell_ref, cell_in), (stream_ref, stream_in), (span_ref, span_in)))
    ]
    load_prop = pltpu.make_async_copy(prop_ref, prop, load_sem.at[4])
    fields = fld.reshape(NF, planes, tall, nz)
    flat = fld.reshape(NF * planes * tall, nz)
    pairs = planes // 2

    def load_pair(i):
        at = pl.multiple_of(2 * lax.rem(peer(0) + (pairs - i) % pairs, pairs), 2)
        return [
            pltpu.make_async_copy(
                ref.at[:, pl.ds(at, 2)],
                fields.at[pl.ds(3 * half, 3), pl.ds(at, 2), pl.ds(PAD, ny), :],
                pair_sem.at[i, half])
            for half, ref in enumerate((adj_ref, base_ref))
        ]

    def wait_pairs(first, last):
        for i in range(first, last):
            for copy in load_pair(i):
                copy.wait()

    def forcing(x, at, rows, put):
        ahead, behind = lax.rem(x + 1, planes), lax.rem(x + planes - 1, planes)
        m = met[pl.ds(at, rows), :]

        def read(f, plane, shift=0):
            return fld[f * planes + plane, pl.ds(PAD + shift + at, rows), :]

        mid = [read(f, x) for f in range(NF)]
        dx = [read(f, ahead) - read(f, behind) for f in range(NF)]
        dy = [read(f, x, 1) - read(f, x, -1) for f in range(NF)]
        dz = [pltpu.roll(mid[f], nz - 1, 1) - pltpu.roll(mid[f], 1, 1) for f in range(NF)]
        b1 = mid[4] * m
        for c in range(3):
            d = (dx, dy, dz)[c]
            stretch = mid[0] * d[3] + mid[1] * d[4] + mid[2] * d[5]
            if c == 1:
                stretch = stretch * m
            advect = mid[3] * dx[c] + b1 * dy[c] + mid[5] * dz[c]
            put(c, mid[c] + 0.125 * (advect - stretch))

    def fill(ref, x, first, rows):
        def put(c, value):
            ref[:, pl.ds(c * nz, nz)] = value

        forcing(x, first, rows, put)

    def fill_edges(ref, x):
        for at, to in ((0, 0), (ny - 8, 8)):
            def put(c, value, to=to):
                ref[pl.ds(to, 8), pl.ds(c * nz, nz)] = value

            forcing(x, at, 8, put)

    def inner_copy(k, j):
        return to_peer(inner_out.at[k, j], inner_in.at[k, w], i_send.at[k, j], i_recv.at[k, j], j)

    def edge_copy(k, j):
        return to_peer(edge_out.at[k, j], edge_in.at[k, w], e_send.at[k, j], e_recv.at[k, j], j)

    y_halo, z_halo = [], []
    for side in range(2):
        step = 1 - 2 * side
        y_halo.append(pltpu.make_async_remote_copy(
            yh_out.at[side], yh_in.at[side], y_send.at[side], y_recv.at[side],
            device_id=(lax.rem(w + WN + step, WN), s), device_id_type=MESH))
        z_halo.append(pltpu.make_async_remote_copy(
            zh_out.at[side], zh_in.at[side], z_send.at[side], z_recv.at[side],
            device_id=(w, lax.rem(s + SP + step, SP)), device_id_type=MESH))
    slot_copies = [
        pltpu.make_async_remote_copy(
            msg, slots.at[o + 1], s_send.at[o], s_recv.at[o], device_id=device, device_id_type=MESH)
        for o, device in enumerate(slot_peers)
    ]
    fix_copies = [to_peer(fix_out.at[j], fix_in.at[w], x_send.at[j], x_recv.at[j], j) for j in range(WN - 1)]
    wall_copies = [
        pltpu.make_async_remote_copy(
            wall_part.at[pl.ds(pl.multiple_of(((s + o + 1) % BLOCK) * 8, 8), 8), :], wall_in.at[o + 1],
            w_send.at[o], w_recv.at[o], device_id=device, device_id_type=MESH)
        for o, device in enumerate(row_peers)
    ]

    def greet():
        for device in greeted:
            pl.semaphore_signal(barrier, inc=1, device_id=device, device_id_type=MESH)

    def start_loads():
        small[0].start()
        for i in range(pairs):
            for copy in load_pair(i):
                copy.start()
        for copy in small[1:] + [load_prop]:
            copy.start()

    def spread_metric():
        small[0].wait()
        here = lax.broadcasted_iota(jnp.int32, (ny, ny), 0) == lax.broadcasted_iota(jnp.int32, (ny, ny), 1)
        column = jnp.sum(jnp.where(here, jnp.broadcast_to(metric_in[...], (ny, ny)), 0.0), 1, keepdims=True)
        met[...] = jnp.broadcast_to(2.0 * column, (ny, nz))

    def build_slots():
        for copy in small[1:]:
            copy.wait()
        alive = lax.broadcasted_iota(jnp.int32, (1, nz), 1) < count_ref[0]
        msg[...] = jnp.concatenate(
            [
                cell_in[...].astype(F32),
                jnp.where(alive, stream_in[...], 0.0),
                jnp.where(alive, span_in[...], 0.0),
                jnp.zeros((MSG - 3, nz), F32),
            ],
            0,
        )
        slots[0] = msg[...]

    def start_slots():
        for copy in slot_copies:
            copy.start()

    def pack_y():
        yh_out[0] = flat[pl.ds(PAD + ny - 1, NF * planes, stride=tall), :]
        yh_out[1] = flat[pl.ds(PAD, NF * planes, stride=tall), :]

    def send_y():
        pl.when(w != WN - 1)(y_halo[0].start)
        pl.when(w != 0)(y_halo[1].start)

    def pack_z():
        def pack(r, carry):
            at = pl.multiple_of(r * 8, 8)
            halves = []
            for half in range(2):
                ends = jnp.zeros((8, nz), F32)
                for i in range(3 * planes):
                    tile = fld[half * 3 * planes + i, pl.ds(PAD + at, 8), :]
                    ends = jnp.where(lane // 2 == i, pltpu.roll(tile, 2 * i + 1, 1), ends)
                ends_own[half, pl.ds(at, 8), :] = ends
                halves.append(ends)
            even = lane % 2 == 0
            zh_out[0, pl.ds(at, 8), :] = jnp.where(even, halves[0], pltpu.roll(halves[1], 1, 1))
            zh_out[1, pl.ds(at, 8), :] = jnp.where(even, pltpu.roll(halves[1], nz - 1, 1), halves[0])
            return carry

        lax.fori_loop(0, blocks, pack, 0)

    def send_z():
        for copy in z_halo:
            copy.start()

    def fill_inner(k, j):
        fill(inner_out.at[k, j], 2 * peer(j) + k, 8, ny - 16)

    def inners(k, first, last):
        def inner(j, carry):
            fill_inner(k, j)
            inner_copy(k, j).start()
            return carry

        lax.fori_loop(first, last, inner, 0)

    def inner_own(k):
        fill(inner_in.at[k, w], 2 * w + k, 8, ny - 16)

    def wait_y():
        for side, (edge_of_wall, row) in enumerate(((0, PAD - 1), (WN - 1, PAD + ny))):
            spot = (pl.ds(row, NF * planes, stride=tall), slice(None))

            @pl.when(w != edge_of_wall)
            def _(side=side, spot=spot):
                y_halo[side].wait_recv()
                flat[spot] = yh_in[side]

            @pl.when(w == edge_of_wall)
            def _(spot=spot):
                flat[spot] = jnp.zeros((NF * planes, nz), F32)

        pl.when(w != WN - 1)(y_halo[0].wait_send)
        pl.when(w != 0)(y_halo[1].wait_send)

    def edges(k):
        def edge(j, carry):
            fill_edges(edge_out.at[k, j], 2 * peer(j) + k)
            edge_copy(k, j).start()
            return carry

        lax.fori_loop(0, WN - 1, edge, 0)
        fill_edges(edge_in.at[k, w], 2 * w + k)

    def send_fix():
        for copy in z_halo:
            copy.wait()
        group = lane // (2 * planes)
        for r in range(blocks):
            rows = pl.ds(8 * r, 8)
            own = [ends_own[half, rows, :] for half in range(2)]
            before, after = zh_in[0, rows, :], zh_in[1, rows, :]
            before = [before, pltpu.roll(before, nz - 1, 1)]
            after = [after, pltpu.roll(after, 1, 1)]
            delta = [
                0.5 * jnp.where(
                    lane % 2 == 0,
                    pltpu.roll(after[half] - own[half], nz - 1, 1),
                    pltpu.roll(own[half] - before[half], 1, 1))
                for half in range(2)
            ]
            b2 = jnp.where(
                group == 0, pltpu.roll(own[1], nz - 4 * planes, 1),
                jnp.where(group == 1, pltpu.roll(own[1], nz - 2 * planes, 1), own[1]))
            each = own[0] * delta[1]
            stretch = each + pltpu.roll(each, 2 * planes, 1) + pltpu.roll(each, 4 * planes, 1)
            fix[r] = 0.25 * (b2 * delta[0] - jnp.where(group == 2, stretch, 0.0))

        def fix_of(to):
            out = jnp.zeros((8, nz), F32)
            for r in range(blocks):
                moved = pltpu.roll(fix[r], (nz + 4 * r - 4 * to) % nz, 1)
                out = jnp.where((lane % (2 * planes)) // 4 == r, moved, out)
            return out

        for j in range(WN - 1):
            fix_out[j] = fix_of(peer(j))
            fix_copies[j].start()
        fix_in[w] = fix_of(w)

    def send_walls():
        for copy in slot_copies:
            copy.wait()
        n = 8 * BLOCK
        for i in range(2 * WN):
            got = slots[i]
            cell = got[0:1].astype(jnp.int32)
            side = cell // (planes * nz * SP)
            left = cell % (planes * nz * SP)
            plane, z = left // (nz * SP), left % (nz * SP)
            tile = z // nz
            ours = (plane // 2 == w) & (tile // BLOCK == s // BLOCK)
            key = jnp.where(ours, (tile % BLOCK) * 4 + (plane % 2) * 2 + side, -1)
            row = lax.broadcasted_iota(jnp.int32, (n, nz), 0)
            parts = [got[1:2], got[2:3]]
            for p in range(3):
                tops = [v.astype(BF16).astype(F32) for v in parts]
                parts = [v - t for v, t in zip(parts, tops)]
                pick = jnp.where(row // 2 == key, jnp.where(row % 2 == 0, tops[0], tops[1]), 0.0)
                pick_rows[pl.ds(p * n, n), pl.ds(i * nz, nz)] = pick.astype(BF16)
            cells = lax.broadcasted_iota(jnp.int32, (nz, nz), 0)
            pick_cells[:, pl.ds(i * nz, nz)] = jnp.where(cells == z % nz, 1.0, 0.0).astype(BF16)
        summed = lax.dot_general(
            pick_rows[...], pick_cells[...], (((1,), (1,)), ((), ())), preferred_element_type=F32)
        wall_part[...] = summed[0:n] + summed[n:2 * n] + summed[2 * n:3 * n]
        for copy in wall_copies:
            copy.start()
        wall_in[0] = wall_part[pl.ds(pl.multiple_of((s % BLOCK) * 8, 8), 8), :]

    def split_prop():
        load_prop.wait()
        whole = prop[...]
        high = whole.astype(BF16)
        prop3[:, pl.ds(0, depth)] = high
        prop3[:, pl.ds(depth, depth)] = (whole - high.astype(F32)).astype(BF16)
        prop3[:, pl.ds(2 * depth, depth)] = high

    def rows_copy(k, j):
        return to_peer(
            rows_out.at[k, :, pl.ds(pl.multiple_of(peer(j) * ny, ny), ny), :], out_ref.at[:, 2 * w + k],
            u_send.at[k, j], u_recv.at[k, j], j)

    greet()
    start_loads()
    spread_metric()
    wait_pairs(0, pairs)
    pack_y()
    fill_inner(0, 0)
    fill_inner(0, 1)
    build_slots()
    pl.semaphore_wait(barrier, len(greeted))
    inner_copy(0, 0).start()
    inner_copy(0, 1).start()
    send_y()
    start_slots()
    inners(0, 2, WN - 1)
    pack_z()
    send_z()
    inner_own(0)
    inners(1, 0, 2)
    wait_y()
    edges(0)
    send_fix()
    send_walls()
    inners(1, 2, WN - 1)
    edges(1)
    inner_own(1)
    split_prop()

    own_copies = []
    for k in range(2):
        for j in range(WN - 1):
            inner_copy(k, j).wait_recv()
            edge_copy(k, j).wait_recv()
        if k == 0:
            for copy in fix_copies + wall_copies:
                copy.wait()
            walls = wall_in[0]
            for o in range(1, BLOCK):
                walls = walls + wall_in[o]
        for side, (device, y) in enumerate(((0, 1), (WN - 1, 6))):
            for comp, c in ((0, 0), (1, 2)):
                at = k * 4 + side * 2 + comp
                spot = (k, device, pl.ds(8 * side, 8), pl.ds(c * nz, nz))
                edge_in[spot] = edge_in[spot] + jnp.where(row8 == y, walls[at:at + 1], 0.0)

        def split(d, carry, k=k):
            ends = edge_in[k, d]
            whole = jnp.concatenate([ends[0:8], inner_in[k, d], ends[8:16]], 0)
            change = fix_in[d]
            fixes = []
            for c in range(3):
                moved = [
                    pltpu.roll(change, (2 * nz - 1 - 2 * planes * c - 4 * r - 2 * k) % nz, 1)
                    for r in range(blocks)
                ]
                fixes.append(jnp.concatenate(
                    [jnp.where((lane == 0) | (lane == nz - 1), v, 0.0) for v in moved], 0))
            whole = whole + jnp.concatenate(fixes, 1)
            high = whole.astype(BF16)
            low = (whole - high.astype(F32)).astype(BF16)
            at = pl.multiple_of(d * ny, ny)
            cols3[pl.ds(at, ny), :] = high
            cols3[pl.ds(depth + at, ny), :] = high
            cols3[pl.ds(2 * depth + at, ny), :] = low
            return carry

        lax.fori_loop(0, WN, split, 0)
        updated = jnp.dot(prop3[...], cols3[...], preferred_element_type=F32)
        for c in range(3):
            rows_out[k, c] = updated[:, c * nz:(c + 1) * nz]
        for j in range(WN - 1):
            rows_copy(k, j).start()
        copy = pltpu.make_async_copy(
            rows_out.at[k, :, pl.ds(pl.multiple_of(w * ny, ny), ny), :], out_ref.at[:, 2 * w + k],
            own_sem.at[k])
        copy.start()
        own_copies.append(copy)
    for k in range(2):
        for j in range(WN - 1):
            inner_copy(k, j).wait_send()
            edge_copy(k, j).wait_send()
    for k in range(2):
        for j in range(WN - 1):
            rows_copy(k, j).wait()
        own_copies[k].wait()


def per_device(
    adjoint, base_flow, metric, propagator, sensor_cell, stream_stress, span_stress, sensor_count
):
    comps, planes, ny, nz = adjoint.shape
    depth = propagator.shape[0]
    hbm = pl.BlockSpec(memory_space=pltpu.HBM)
    dma = pltpu.SemaphoreType.DMA
    return pl.pallas_call(
        kernel,
        name="substep",
        out_shape=jax.ShapeDtypeStruct(adjoint.shape, F32),
        in_specs=[hbm] * 7 + [pl.BlockSpec(memory_space=pltpu.SMEM)],
        out_specs=pl.BlockSpec(memory_space=pl.ANY),
        scratch_shapes=[
            pltpu.VMEM((1, ny), F32),
            pltpu.VMEM((1, nz), jnp.int32),
            pltpu.VMEM((1, nz), F32),
            pltpu.VMEM((1, nz), F32),
            pltpu.VMEM((NF * planes, ny + 2 * PAD, nz), F32),
            pltpu.VMEM((2, NF * planes, nz), F32),
            pltpu.VMEM((2, NF * planes, nz), F32),
            pltpu.VMEM((2, ny, nz), F32),
            pltpu.VMEM((2, ny, nz), F32),
            pltpu.VMEM((2, ny, nz), F32),
            pltpu.VMEM((ny // 8, 8, nz), F32),
            pltpu.VMEM((WN - 1, 8, nz), F32),
            pltpu.VMEM((WN, 8, nz), F32),
            pltpu.VMEM((ny, nz), F32),
            pltpu.VMEM((2, WN - 1, ny - 16, comps * nz), F32),
            pltpu.VMEM((2, WN - 1, 16, comps * nz), F32),
            pltpu.VMEM((2, WN, ny - 16, comps * nz), F32),
            pltpu.VMEM((2, WN, 16, comps * nz), F32),
            pltpu.VMEM((3 * depth, comps * nz), BF16),
            pltpu.VMEM((depth, depth), F32),
            pltpu.VMEM((depth, 3 * depth), BF16),
            pltpu.VMEM((2, comps, depth, nz), F32),
            pltpu.VMEM((MSG, nz), F32),
            pltpu.VMEM((2 * WN, MSG, nz), F32),
            pltpu.VMEM((24 * BLOCK, 2 * WN * nz), BF16),
            pltpu.VMEM((nz, 2 * WN * nz), BF16),
            pltpu.VMEM((8 * BLOCK, nz), F32),
            pltpu.VMEM((BLOCK, 8, nz), F32),
            dma((5,)), dma((planes // 2, 2)),
            dma((2,)), dma((2,)), dma((2,)), dma((2,)),
            dma((WN - 1,)), dma((WN - 1,)),
            *([dma((2, WN - 1))] * 6), dma((2,)),
            dma((2 * WN - 1,)), dma((2 * WN - 1,)), dma((BLOCK - 1,)), dma((BLOCK - 1,)),
        ],
        compiler_params=pltpu.CompilerParams(
            collective_id=0, has_side_effects=True, vmem_limit_bytes=48 << 20),
    )(
        *(pltpu.with_memory_space_constraint(a, pltpu.HBM) for a in (
            adjoint,
            base_flow,
            metric.reshape(1, ny),
            propagator,
            sensor_cell.reshape(1, nz),
            stream_stress.reshape(1, nz),
            span_stress.reshape(1, nz),
        )),
        sensor_count,
    )


def solution(mesh):
    placed = (
        P(None, None, "wn", "sp"),
        P(None, None, "wn", "sp"),
        P("wn"),
        P(),
        P(("wn", "sp")),
        P(("wn", "sp")),
        P(("wn", "sp")),
        P(("wn", "sp")),
    )
    return jax.shard_map(
        per_device, mesh=mesh, in_specs=placed, out_specs=P(None, None, "wn", "sp"), check_vma=False
    )
```

```python
import jax
import jax.numpy as jnp
from jax import lax
from jax.experimental import pallas as pl
from jax.experimental.pallas import tpu as pltpu
from jax.sharding import PartitionSpec as P

MESH = pl.DeviceIdType.MESH
BF16 = jnp.bfloat16
F32 = jnp.float32

MSG = 4
NF = 6
PAD = 8
WN = 8
SP = 16
BLOCK = 8


def kernel(
    adj_ref, base_ref, metric_ref, prop_ref, cell_ref, stream_ref, span_ref, count_ref,
    out_ref,
    metric_in, cell_in, stream_in, span_in,
    fld, yh_out, yh_in, ends_own, zh_out, zh_in, fix, fix_out, fix_in, met,
    inner_out, edge_out, inner_in, edge_in, cols3, prop, prop3, rows_out,
    msg, slots, pick_rows, pick_cells, wall_part, wall_in,
    load_sem, pair_sem, y_send, y_recv, z_send, z_recv, x_send, x_recv, i_send, i_recv, e_send, e_recv,
    u_send, u_recv, own_sem, s_send, s_recv, w_send, w_recv,
):
    planes = out_ref.shape[1]
    ny = out_ref.shape[2]
    nz = out_ref.shape[3]
    tall = ny + 2 * PAD
    blocks = ny // 8
    depth = prop.shape[1]
    w = lax.axis_index("wn")
    s = lax.axis_index("sp")
    lane = lax.broadcasted_iota(jnp.int32, (8, nz), 1)
    row8 = lax.broadcasted_iota(jnp.int32, (8, nz), 0)

    mirror = 1 - 2 * lax.rem(s, 2)
    half, along = lax.div(w, 4), lax.rem(w, 4) + 4
    steps = ((2, 1), (1, 1), (-1, 0), (0, 1), (-1, 1), (1, 0), (2, 0), (0, 0))

    def peer(j):
        if isinstance(j, int):
            dy, dz = steps[j]
        else:
            dy, dz = 0, 0
            for i, (y, z) in enumerate(steps):
                dy, dz = jnp.where(j == i, y, dy), jnp.where(j == i, z, dz)
        return lax.rem(half + dz, 2) * 4 + lax.rem(along + dy * mirror, 4)

    def to_peer(src, dst, send, recv, j):
        return pltpu.make_async_remote_copy(
            src, dst, send, recv, device_id=(peer(j), s), device_id_type=MESH)

    barrier = pltpu.get_barrier_semaphore()
    base = s - lax.rem(s, BLOCK)
    row_peers = [(w, base + lax.rem(s + o, BLOCK)) for o in range(1, BLOCK)]
    across = lax.rem(s + BLOCK, SP)
    slot_peers = [(lax.rem(w + o, WN), across if o >= WN else s) for o in range(1, 2 * WN)]
    greeted = row_peers + slot_peers + [(w, lax.rem(s + 1, SP)), (w, lax.rem(s + SP - 1, SP))]

    small = [
        pltpu.make_async_copy(src, dst, load_sem.at[i])
        for i, (src, dst) in enumerate((
            (metric_ref, metric_in), (cell_ref, cell_in), (stream_ref, stream_in), (span_ref, span_in)))
    ]
    load_prop = pltpu.make_async_copy(prop_ref, prop, load_sem.at[4])
    fields = fld.reshape(NF, planes, tall, nz)
    flat = fld.reshape(NF * planes * tall, nz)
    pairs = planes // 2

    def load_pair(i):
        at = pl.multiple_of(2 * lax.rem(peer(0) + (pairs - i) % pairs, pairs), 2)
        return [
            pltpu.make_async_copy(
                ref.at[:, pl.ds(at, 2)],
                fields.at[pl.ds(3 * half, 3), pl.ds(at, 2), pl.ds(PAD, ny), :],
                pair_sem.at[i, half])
            for half, ref in enumerate((adj_ref, base_ref))
        ]

    def wait_pairs(first, last):
        for i in range(first, last):
            for copy in load_pair(i):
                copy.wait()

    def forcing(x, at, rows, put):
        ahead, behind = lax.rem(x + 1, planes), lax.rem(x + planes - 1, planes)
        m = met[pl.ds(at, rows), :]

        def read(f, plane, shift=0):
            return fld[f * planes + plane, pl.ds(PAD + shift + at, rows), :]

        mid = [read(f, x) for f in range(NF)]
        dx = [read(f, ahead) - read(f, behind) for f in range(NF)]
        dy = [read(f, x, 1) - read(f, x, -1) for f in range(NF)]
        dz = [pltpu.roll(mid[f], nz - 1, 1) - pltpu.roll(mid[f], 1, 1) for f in range(NF)]
        b1 = mid[4] * m
        for c in range(3):
            d = (dx, dy, dz)[c]
            stretch = mid[0] * d[3] + mid[1] * d[4] + mid[2] * d[5]
            if c == 1:
                stretch = stretch * m
            advect = mid[3] * dx[c] + b1 * dy[c] + mid[5] * dz[c]
            put(c, mid[c] + 0.125 * (advect - stretch))

    def fill(ref, x, first, rows):
        def put(c, value):
            ref[:, pl.ds(c * nz, nz)] = value

        forcing(x, first, rows, put)

    def fill_edges(ref, x):
        for at, to in ((0, 0), (ny - 8, 8)):
            def put(c, value, to=to):
                ref[pl.ds(to, 8), pl.ds(c * nz, nz)] = value

            forcing(x, at, 8, put)

    def inner_copy(k, j):
        return to_peer(inner_out.at[k, j], inner_in.at[k, w], i_send.at[k, j], i_recv.at[k, j], j)

    def edge_copy(k, j):
        return to_peer(edge_out.at[k, j], edge_in.at[k, w], e_send.at[k, j], e_recv.at[k, j], j)

    y_halo, z_halo = [], []
    for side in range(2):
        step = 1 - 2 * side
        y_halo.append(pltpu.make_async_remote_copy(
            yh_out.at[side], yh_in.at[side], y_send.at[side], y_recv.at[side],
            device_id=(lax.rem(w + WN + step, WN), s), device_id_type=MESH))
        z_halo.append(pltpu.make_async_remote_copy(
            zh_out.at[side], zh_in.at[side], z_send.at[side], z_recv.at[side],
            device_id=(w, lax.rem(s + SP + step, SP)), device_id_type=MESH))
    slot_copies = [
        pltpu.make_async_remote_copy(
            msg, slots.at[o + 1], s_send.at[o], s_recv.at[o], device_id=device, device_id_type=MESH)
        for o, device in enumerate(slot_peers)
    ]
    fix_copies = [to_peer(fix_out.at[j], fix_in.at[w], x_send.at[j], x_recv.at[j], j) for j in range(WN - 1)]
    wall_copies = [
        pltpu.make_async_remote_copy(
            wall_part.at[pl.ds(pl.multiple_of(((s + o + 1) % BLOCK) * 8, 8), 8), :], wall_in.at[o + 1],
            w_send.at[o], w_recv.at[o], device_id=device, device_id_type=MESH)
        for o, device in enumerate(row_peers)
    ]

    def greet():
        for device in greeted:
            pl.semaphore_signal(barrier, inc=1, device_id=device, device_id_type=MESH)

    def start_loads():
        small[0].start()
        for i in range(pairs):
            for copy in load_pair(i):
                copy.start()
        for copy in small[1:] + [load_prop]:
            copy.start()

    def spread_metric():
        small[0].wait()
        here = lax.broadcasted_iota(jnp.int32, (ny, ny), 0) == lax.broadcasted_iota(jnp.int32, (ny, ny), 1)
        column = jnp.sum(jnp.where(here, jnp.broadcast_to(metric_in[...], (ny, ny)), 0.0), 1, keepdims=True)
        met[...] = jnp.broadcast_to(2.0 * column, (ny, nz))

    def build_slots():
        for copy in small[1:]:
            copy.wait()
        alive = lax.broadcasted_iota(jnp.int32, (1, nz), 1) < count_ref[0]
        msg[...] = jnp.concatenate(
            [
                cell_in[...].astype(F32),
                jnp.where(alive, stream_in[...], 0.0),
                jnp.where(alive, span_in[...], 0.0),
                jnp.zeros((MSG - 3, nz), F32),
            ],
            0,
        )
        slots[0] = msg[...]

    def start_slots():
        for copy in slot_copies:
            copy.start()

    def pack_y():
        yh_out[0] = flat[pl.ds(PAD + ny - 1, NF * planes, stride=tall), :]
        yh_out[1] = flat[pl.ds(PAD, NF * planes, stride=tall), :]

    def send_y():
        pl.when(w != WN - 1)(y_halo[0].start)
        pl.when(w != 0)(y_halo[1].start)

    def pack_z():
        def pack(r, carry):
            at = pl.multiple_of(r * 8, 8)
            halves = []
            for half in range(2):
                ends = jnp.zeros((8, nz), F32)
                for i in range(3 * planes):
                    tile = fld[half * 3 * planes + i, pl.ds(PAD + at, 8), :]
                    ends = jnp.where(lane // 2 == i, pltpu.roll(tile, 2 * i + 1, 1), ends)
                ends_own[half, pl.ds(at, 8), :] = ends
                halves.append(ends)
            even = lane % 2 == 0
            zh_out[0, pl.ds(at, 8), :] = jnp.where(even, halves[0], pltpu.roll(halves[1], 1, 1))
            zh_out[1, pl.ds(at, 8), :] = jnp.where(even, pltpu.roll(halves[1], nz - 1, 1), halves[0])
            return carry

        lax.fori_loop(0, blocks, pack, 0)

    def send_z():
        for copy in z_halo:
            copy.start()

    def fill_inner(k, j):
        fill(inner_out.at[k, j], 2 * peer(j) + k, 8, ny - 16)

    def inners(k, first, last):
        def inner(j, carry):
            fill_inner(k, j)
            inner_copy(k, j).start()
            return carry

        lax.fori_loop(first, last, inner, 0)

    def inner_own(k):
        fill(inner_in.at[k, w], 2 * w + k, 8, ny - 16)

    def wait_y():
        for side, (edge_of_wall, row) in enumerate(((0, PAD - 1), (WN - 1, PAD + ny))):
            spot = (pl.ds(row, NF * planes, stride=tall), slice(None))

            @pl.when(w != edge_of_wall)
            def _(side=side, spot=spot):
                y_halo[side].wait_recv()
                flat[spot] = yh_in[side]

            @pl.when(w == edge_of_wall)
            def _(spot=spot):
                flat[spot] = jnp.zeros((NF * planes, nz), F32)

        pl.when(w != WN - 1)(y_halo[0].wait_send)
        pl.when(w != 0)(y_halo[1].wait_send)

    def edges(k):
        def edge(j, carry):
            fill_edges(edge_out.at[k, j], 2 * peer(j) + k)
            edge_copy(k, j).start()
            return carry

        lax.fori_loop(0, WN - 1, edge, 0)
        fill_edges(edge_in.at[k, w], 2 * w + k)

    def send_fix():
        for copy in z_halo:
            copy.wait()
        group = lane // (2 * planes)
        for r in range(blocks):
            rows = pl.ds(8 * r, 8)
            own = [ends_own[half, rows, :] for half in range(2)]
            before, after = zh_in[0, rows, :], zh_in[1, rows, :]
            before = [before, pltpu.roll(before, nz - 1, 1)]
            after = [after, pltpu.roll(after, 1, 1)]
            delta = [
                0.5 * jnp.where(
                    lane % 2 == 0,
                    pltpu.roll(after[half] - own[half], nz - 1, 1),
                    pltpu.roll(own[half] - before[half], 1, 1))
                for half in range(2)
            ]
            b2 = jnp.where(
                group == 0, pltpu.roll(own[1], nz - 4 * planes, 1),
                jnp.where(group == 1, pltpu.roll(own[1], nz - 2 * planes, 1), own[1]))
            each = own[0] * delta[1]
            stretch = each + pltpu.roll(each, 2 * planes, 1) + pltpu.roll(each, 4 * planes, 1)
            fix[r] = 0.25 * (b2 * delta[0] - jnp.where(group == 2, stretch, 0.0))

        def fix_of(to):
            out = jnp.zeros((8, nz), F32)
            for r in range(blocks):
                moved = pltpu.roll(fix[r], (nz + 4 * r - 4 * to) % nz, 1)
                out = jnp.where((lane % (2 * planes)) // 4 == r, moved, out)
            return out

        for j in range(WN - 1):
            fix_out[j] = fix_of(peer(j))
            fix_copies[j].start()
        fix_in[w] = fix_of(w)

    def send_walls():
        for copy in slot_copies:
            copy.wait()
        n = 8 * BLOCK
        for i in range(2 * WN):
            got = slots[i]
            cell = got[0:1].astype(jnp.int32)
            side = cell // (planes * nz * SP)
            left = cell % (planes * nz * SP)
            plane, z = left // (nz * SP), left % (nz * SP)
            tile = z // nz
            ours = (plane // 2 == w) & (tile // BLOCK == s // BLOCK)
            key = jnp.where(ours, (tile % BLOCK) * 4 + (plane % 2) * 2 + side, -1)
            row = lax.broadcasted_iota(jnp.int32, (n, nz), 0)
            parts = [got[1:2], got[2:3]]
            for p in range(3):
                tops = [v.astype(BF16).astype(F32) for v in parts]
                parts = [v - t for v, t in zip(parts, tops)]
                pick = jnp.where(row // 2 == key, jnp.where(row % 2 == 0, tops[0], tops[1]), 0.0)
                pick_rows[pl.ds(p * n, n), pl.ds(i * nz, nz)] = pick.astype(BF16)
            cells = lax.broadcasted_iota(jnp.int32, (nz, nz), 0)
            pick_cells[:, pl.ds(i * nz, nz)] = jnp.where(cells == z % nz, 1.0, 0.0).astype(BF16)
        summed = lax.dot_general(
            pick_rows[...], pick_cells[...], (((1,), (1,)), ((), ())), preferred_element_type=F32)
        wall_part[...] = summed[0:n] + summed[n:2 * n] + summed[2 * n:3 * n]
        for copy in wall_copies:
            copy.start()
        wall_in[0] = wall_part[pl.ds(pl.multiple_of((s % BLOCK) * 8, 8), 8), :]

    def split_prop():
        load_prop.wait()
        whole = prop[...]
        high = whole.astype(BF16)
        prop3[:, pl.ds(0, depth)] = high
        prop3[:, pl.ds(depth, depth)] = (whole - high.astype(F32)).astype(BF16)
        prop3[:, pl.ds(2 * depth, depth)] = high

    def rows_copy(k, j):
        return to_peer(
            rows_out.at[k, :, pl.ds(pl.multiple_of(peer(j) * ny, ny), ny), :], out_ref.at[:, 2 * w + k],
            u_send.at[k, j], u_recv.at[k, j], j)

    greet()
    start_loads()
    spread_metric()
    wait_pairs(0, pairs)
    pack_y()
    fill_inner(0, 0)
    fill_inner(0, 1)
    build_slots()
    pl.semaphore_wait(barrier, len(greeted))
    inner_copy(0, 0).start()
    inner_copy(0, 1).start()
    send_y()
    start_slots()
    inners(0, 2, WN - 1)
    pack_z()
    send_z()
    inner_own(0)
    inners(1, 0, 2)
    wait_y()
    edges(0)
    send_fix()
    send_walls()
    inners(1, 2, WN - 1)
    edges(1)
    inner_own(1)
    split_prop()

    own_copies = []
    for k in range(2):
        for j in range(WN - 1):
            inner_copy(k, j).wait_recv()
            edge_copy(k, j).wait_recv()
        if k == 0:
            for copy in fix_copies + wall_copies:
                copy.wait()
            walls = wall_in[0]
            for o in range(1, BLOCK):
                walls = walls + wall_in[o]
        for side, (device, y) in enumerate(((0, 1), (WN - 1, 6))):
            for comp, c in ((0, 0), (1, 2)):
                at = k * 4 + side * 2 + comp
                spot = (k, device, pl.ds(8 * side, 8), pl.ds(c * nz, nz))
                edge_in[spot] = edge_in[spot] + jnp.where(row8 == y, walls[at:at + 1], 0.0)

        def split(d, carry, k=k):
            ends = edge_in[k, d]
            whole = jnp.concatenate([ends[0:8], inner_in[k, d], ends[8:16]], 0)
            change = fix_in[d]
            fixes = []
            for c in range(3):
                moved = [
                    pltpu.roll(change, (2 * nz - 1 - 2 * planes * c - 4 * r - 2 * k) % nz, 1)
                    for r in range(blocks)
                ]
                fixes.append(jnp.concatenate(
                    [jnp.where((lane == 0) | (lane == nz - 1), v, 0.0) for v in moved], 0))
            whole = whole + jnp.concatenate(fixes, 1)
            high = whole.astype(BF16)
            low = (whole - high.astype(F32)).astype(BF16)
            at = pl.multiple_of(d * ny, ny)
            cols3[pl.ds(at, ny), :] = high
            cols3[pl.ds(depth + at, ny), :] = high
            cols3[pl.ds(2 * depth + at, ny), :] = low
            return carry

        lax.fori_loop(0, WN, split, 0)
        updated = jnp.dot(prop3[...], cols3[...], preferred_element_type=F32)
        for c in range(3):
            rows_out[k, c] = updated[:, c * nz:(c + 1) * nz]
        for j in range(WN - 1):
            rows_copy(k, j).start()
        copy = pltpu.make_async_copy(
            rows_out.at[k, :, pl.ds(pl.multiple_of(w * ny, ny), ny), :], out_ref.at[:, 2 * w + k],
            own_sem.at[k])
        copy.start()
        own_copies.append(copy)
    for k in range(2):
        for j in range(WN - 1):
            inner_copy(k, j).wait_send()
            edge_copy(k, j).wait_send()
    for k in range(2):
        for j in range(WN - 1):
            rows_copy(k, j).wait()
        own_copies[k].wait()


def per_device(
    adjoint, base_flow, metric, propagator, sensor_cell, stream_stress, span_stress, sensor_count
):
    comps, planes, ny, nz = adjoint.shape
    depth = propagator.shape[0]
    hbm = pl.BlockSpec(memory_space=pltpu.HBM)
    dma = pltpu.SemaphoreType.DMA
    return pl.pallas_call(
        kernel,
        name="substep",
        out_shape=jax.ShapeDtypeStruct(adjoint.shape, F32),
        in_specs=[hbm] * 7 + [pl.BlockSpec(memory_space=pltpu.SMEM)],
        out_specs=pl.BlockSpec(memory_space=pl.ANY),
        scratch_shapes=[
            pltpu.VMEM((1, ny), F32),
            pltpu.VMEM((1, nz), jnp.int32),
            pltpu.VMEM((1, nz), F32),
            pltpu.VMEM((1, nz), F32),
            pltpu.VMEM((NF * planes, ny + 2 * PAD, nz), F32),
            pltpu.VMEM((2, NF * planes, nz), F32),
            pltpu.VMEM((2, NF * planes, nz), F32),
            pltpu.VMEM((2, ny, nz), F32),
            pltpu.VMEM((2, ny, nz), F32),
            pltpu.VMEM((2, ny, nz), F32),
            pltpu.VMEM((ny // 8, 8, nz), F32),
            pltpu.VMEM((WN - 1, 8, nz), F32),
            pltpu.VMEM((WN, 8, nz), F32),
            pltpu.VMEM((ny, nz), F32),
            pltpu.VMEM((2, WN - 1, ny - 16, comps * nz), F32),
            pltpu.VMEM((2, WN - 1, 16, comps * nz), F32),
            pltpu.VMEM((2, WN, ny - 16, comps * nz), F32),
            pltpu.VMEM((2, WN, 16, comps * nz), F32),
            pltpu.VMEM((3 * depth, comps * nz), BF16),
            pltpu.VMEM((depth, depth), F32),
            pltpu.VMEM((depth, 3 * depth), BF16),
            pltpu.VMEM((2, comps, depth, nz), F32),
            pltpu.VMEM((MSG, nz), F32),
            pltpu.VMEM((2 * WN, MSG, nz), F32),
            pltpu.VMEM((24 * BLOCK, 2 * WN * nz), BF16),
            pltpu.VMEM((nz, 2 * WN * nz), BF16),
            pltpu.VMEM((8 * BLOCK, nz), F32),
            pltpu.VMEM((BLOCK, 8, nz), F32),
            dma((5,)), dma((planes // 2, 2)),
            dma((2,)), dma((2,)), dma((2,)), dma((2,)),
            dma((WN - 1,)), dma((WN - 1,)),
            *([dma((2, WN - 1))] * 6), dma((2,)),
            dma((2 * WN - 1,)), dma((2 * WN - 1,)), dma((BLOCK - 1,)), dma((BLOCK - 1,)),
        ],
        compiler_params=pltpu.CompilerParams(
            collective_id=0, has_side_effects=True, vmem_limit_bytes=48 << 20),
    )(
        *(pltpu.with_memory_space_constraint(a, pltpu.HBM) for a in (
            adjoint,
            base_flow,
            metric.reshape(1, ny),
            propagator,
            sensor_cell.reshape(1, nz),
            stream_stress.reshape(1, nz),
            span_stress.reshape(1, nz),
        )),
        sensor_count,
    )


def solution(mesh):
    placed = (
        P(None, None, "wn", "sp"),
        P(None, None, "wn", "sp"),
        P("wn"),
        P(),
        P(("wn", "sp")),
        P(("wn", "sp")),
        P(("wn", "sp")),
        P(("wn", "sp")),
    )
    return jax.shard_map(
        per_device, mesh=mesh, in_specs=placed, out_specs=P(None, None, "wn", "sp"), check_vma=False
    )
```
